128 devices in a mesh: dp: 8 (over z, core), fsdp: 16 (over y, x).
Axes of the slice: x: 4, y: 4, z: 4, core: 2. Of those that a mesh axis runs over, the one named last changes fastest.
Arguments:
- tokens: bfloat16 [256, 256, 384], P(('dp', 'fsdp')), may hold values from -6 to 6
- cotangent: bfloat16 [256, 256, 384], P(('dp', 'fsdp')), may hold values from -6 to 6
- labels: int32 [256], P(('dp', 'fsdp')), may hold values from 0 to 999
- timesteps: int32 [256], P(('dp', 'fsdp')), may hold values from 0 to 999
- counts: int32 [128], P(('dp', 'fsdp')), may hold values from 0 to 2, as said below
- class_table: bfloat16 [1000, 384], replicated, may hold values from -6 to 6
- time_table: bfloat16 [1000, 384], replicated, may hold values from -6 to 6
- ada_weight: float32 [384, 2304], P(None, ('dp', 'fsdp')), may hold values from -0.3125 to 0.3125
- qkv_weight: float32 [384, 1152], P(None, ('dp', 'fsdp')), may hold values from -0.3125 to 0.3125
- out_weight: float32 [384, 384], P(None, ('dp', 'fsdp')), may hold values from -1.75 to 1.75
- up_weight: float32 [384, 1536], P(None, ('dp', 'fsdp')), may hold values from -0.3125 to 0.3125
- down_weight: float32 [1536, 384], P(('dp', 'fsdp')), may hold values from -0.15625 to 0.15625
- biases: float32 [5376], P(('dp', 'fsdp')), may hold values from -3 to 3
- ada_moment: float32 [384, 2304], P(None, ('dp', 'fsdp')), may hold values from -977.5044 to 977.5044
- qkv_moment: float32 [384, 1152], P(None, ('dp', 'fsdp')), may hold values from -977.5044 to 977.5044
- out_moment: float32 [384, 384], P(None, ('dp', 'fsdp')), may hold values from -977.5044 to 977.5044
- up_moment: float32 [384, 1536], P(None, ('dp', 'fsdp')), may hold values from -977.5044 to 977.5044
- down_moment: float32 [1536, 384], P(('dp', 'fsdp')), may hold values from -977.5044 to 977.5044
- bias_moment: float32 [5376], P(('dp', 'fsdp')), may hold values from -448 to 448
Outputs:
- output: bfloat16 [256, 256, 384], P(('dp', 'fsdp'))
- input_grad: float32 [256, 256, 384], P(('dp', 'fsdp'))
- cond_grad: float32 [256, 384], P(('dp', 'fsdp'))
- ada_grad: float32 [384, 2304], P(None, ('dp', 'fsdp'))
- qkv_grad: float32 [384, 1152], P(None, ('dp', 'fsdp'))
- out_grad: float32 [384, 384], P(None, ('dp', 'fsdp'))
- up_grad: float32 [384, 1536], P(None, ('dp', 'fsdp'))
- down_grad: float32 [1536, 384], P(('dp', 'fsdp'))
- bias_grad: float32 [5376], P(('dp', 'fsdp'))
- ada_new: float32 [384, 2304], P(None, ('dp', 'fsdp'))
- qkv_new: float32 [384, 1152], P(None, ('dp', 'fsdp'))
- out_new: float32 [384, 384], P(None, ('dp', 'fsdp'))
- up_new: float32 [384, 1536], P(None, ('dp', 'fsdp'))
- down_new: float32 [1536, 384], P(('dp', 'fsdp'))
- bias_new: float32 [5376], P(('dp', 'fsdp'))
- ada_moment_new: float32 [384, 2304], P(None, ('dp', 'fsdp'))
- qkv_moment_new: float32 [384, 1152], P(None, ('dp', 'fsdp'))
- out_moment_new: float32 [384, 384], P(None, ('dp', 'fsdp'))
- up_moment_new: float32 [384, 1536], P(None, ('dp', 'fsdp'))
- down_moment_new: float32 [1536, 384], P(('dp', 'fsdp'))
- bias_moment_new: float32 [5376], P(('dp', 'fsdp'))
The draws below stay inside these ranges and needn't reach their ends.
Inputs may be any that keep to these rules, and one draw needn't show every extreme that they name: Slot i of device d is live when i < counts[d]; some device has 2 live latents and some none.
All inputs are finite; a program needn't handle non-finite values.
Results may differ from the reference program's by a relative error of at most 0.013.
The reference program's roundings to bfloat16 on the way count: a program that leaves them out, or rounds other values in their place, can miss the bound.
Values may be sent and summed in bfloat16 or wider, within the bound.
No kernel may reach another device: no remote copies, remote signals or barrier semaphores. Data moves between devices by JAX's collectives and lax.ppermute only.
A program may use at most 128 MiB of HBM per device.

```python
import math
import jax
import jax.numpy as jnp
from jax import lax

D = 384
FF = 1536
CLASSES = 1000
HEAD = 64
TSTEPS = 1000
SEQ = 256
LAT_DEV = 2
HEADS = 6
SLOTS = 256
TOKENS = 65536
NBIAS = 5376
N_DP = 8
N_FSDP = 16


def rising(noise, axis, top, base):
    length = noise.shape[axis]
    ramp = jnp.arange(length, dtype=jnp.float32) / max(length - 1, 1)
    growth = jnp.exp(ramp * math.log(top))
    layout = [1, 1]
    layout[axis] = length
    return (base * noise * growth.reshape(layout)).astype(jnp.float32)


def moment_scale():
    return 0.3 * math.sqrt(TOKENS // 2)


def draw_counts(key, part):
    key = jax.random.fold_in(key, 1)
    first_key, second_key = jax.random.split(key)
    drawn = jax.random.randint(first_key, (N_DP * N_FSDP,), 0, LAT_DEV + 1)
    chosen = jax.random.permutation(second_key, N_DP * N_FSDP)
    drawn = drawn.at[chosen[0]].set(LAT_DEV)
    return drawn.at[chosen[1]].set(0).astype(jnp.int32)


def draw_ada_moment(key, part):
    key = jax.random.fold_in(key, 2)
    noise = jax.random.truncated_normal(key, -6.0, 6.0, (D, 6 * D), jnp.float32)
    return rising(noise, 1, 3.0, moment_scale())


def draw_qkv_moment(key, part):
    key = jax.random.fold_in(key, 3)
    noise = jax.random.truncated_normal(key, -6.0, 6.0, (D, 3 * D), jnp.float32)
    return rising(noise, 1, 3.0, moment_scale())


def draw_out_moment(key, part):
    key = jax.random.fold_in(key, 4)
    noise = jax.random.truncated_normal(key, -6.0, 6.0, (D, D), jnp.float32)
    return rising(noise, 1, 3.0, moment_scale())


def draw_up_moment(key, part):
    key = jax.random.fold_in(key, 5)
    noise = jax.random.truncated_normal(key, -6.0, 6.0, (D, FF), jnp.float32)
    return rising(noise, 1, 3.0, moment_scale())


def draw_down_moment(key, part):
    key = jax.random.fold_in(key, 6)
    noise = jax.random.truncated_normal(key, -6.0, 6.0, (FF, D), jnp.float32)
    return rising(noise, 0, 3.0, moment_scale())


def set_ends(values, stream_key, least, high):
    extent = values.shape
    place = [jax.random.randint(jax.random.fold_in(stream_key, axis), (), 0, extent[axis]) for axis in range(len(extent))]
    values = values.at[tuple(place)].set(least)
    longest = extent.index(max(extent))
    place[longest] = (place[longest] + 1) % extent[longest]
    return values.at[tuple(place)].set(high)


def levels(own_key, extent, cuts, low, largest):
    level = 1.0
    for axis_at, parts in cuts:
        draws = jax.random.uniform(jax.random.fold_in(jax.random.fold_in(own_key, 6), axis_at), (parts,), jnp.float32, low / len(cuts), largest / len(cuts))
        level = level * jnp.repeat(jnp.exp(draws), extent[axis_at] // parts).reshape((-1,) + (1,) * (len(extent) - 1 - axis_at))
    return level


def bell_draw(own_key, extent, scale, bound, cuts=(), held_as=jnp.bfloat16):
    loudness = levels(own_key, extent, cuts, -0.22, 0.18) if cuts else 1.0
    entries = jax.random.normal(own_key, extent, jnp.float32) * scale * loudness
    return jnp.minimum(jnp.maximum(entries, -bound), bound).astype(held_as)


def setup_inputs(seed: int = 0) -> dict:
    seeds = jax.random.split(jax.random.key(seed), 20)
    return {
        "tokens": bell_draw(seeds[0], (SLOTS, SEQ, D), 1.0, 6.0, ((0, 128),)),
        "cotangent": bell_draw(seeds[1], (SLOTS, SEQ, D), 1.0, 6.0, ((0, 128),)),
        "labels": set_ends(jax.random.randint(seeds[2], (SLOTS,), 0, CLASSES), jax.random.fold_in(seeds[2], 1), 0, CLASSES - 1).astype(jnp.int32),
        "timesteps": set_ends(jax.random.randint(seeds[3], (SLOTS,), 0, TSTEPS), jax.random.fold_in(seeds[3], 1), 0, TSTEPS - 1).astype(jnp.int32),
        "counts": draw_counts(jax.random.fold_in(seeds[19], 71), 0),
        "class_table": bell_draw(seeds[5], (CLASSES, D), 1.0, 6.0),
        "time_table": bell_draw(seeds[6], (TSTEPS, D), 1.0, 6.0),
        "ada_weight": bell_draw(seeds[7], (D, 6 * D), D ** -0.5, 0.3125, ((1, 128),), jnp.float32),
        "qkv_weight": bell_draw(seeds[8], (D, 3 * D), D ** -0.5, 0.3125, ((1, 128),), jnp.float32),
        "out_weight": bell_draw(seeds[9], (D, D), (D // 32) ** -0.5, 1.75, ((1, 128),), jnp.float32),
        "up_weight": bell_draw(seeds[10], (D, FF), D ** -0.5, 0.3125, ((1, 128),), jnp.float32),
        "down_weight": bell_draw(seeds[11], (FF, D), FF ** -0.5, 0.15625, ((0, 128),), jnp.float32),
        "biases": bell_draw(seeds[12], (NBIAS,), 0.2, 3.0, ((0, 128),), jnp.float32),
        "ada_moment": draw_ada_moment(jax.random.fold_in(seeds[19], 71), 0),
        "qkv_moment": draw_qkv_moment(jax.random.fold_in(seeds[19], 71), 0),
        "out_moment": draw_out_moment(jax.random.fold_in(seeds[19], 71), 0),
        "up_moment": draw_up_moment(jax.random.fold_in(seeds[19], 71), 0),
        "down_moment": draw_down_moment(jax.random.fold_in(seeds[19], 71), 0),
        "bias_moment": bell_draw(seeds[18], (NBIAS,), (0.4 * (TOKENS // 2) ** 0.5), 448.0, ((0, 128),), jnp.float32),
    }


MOMENTUM = 0.95
STEP_RATE = 1.2
BIAS_RATE = 0.3
EPS_NORM = 1e-06
EPS_FRAME = 1e-07
COEF_A = 3.4445
COEF_B = -4.775
COEF_C = 2.0315
HIGH = lax.Precision.HIGHEST

@jax.custom_vjp
def low(v):
    return lax.optimization_barrier(v.astype(jnp.bfloat16)).astype(jnp.float32)

@jax.custom_vjp
def low_back(v):
    return v

def low_keep(v):
    return (low(v), None)

def low_pass(kept, grad):
    return (grad,)

def back_keep(v):
    return (v, None)

def back_low(kept, grad):
    return (low(grad),)
low.defvjp(low_keep, low_pass)
low_back.defvjp(back_keep, back_low)

def layer_norm(vectors):
    centred = vectors - lax.optimization_barrier(jnp.mean(vectors, axis=-1, keepdims=True))
    spread = lax.optimization_barrier(jnp.mean(centred * centred, axis=-1, keepdims=True))
    return centred * lax.rsqrt(spread + EPS_NORM)

def newton_step(matrix, gram_matrix):
    mixed_terms = COEF_B * gram_matrix + COEF_C * jnp.dot(gram_matrix, gram_matrix, precision=HIGH)
    return COEF_A * matrix + jnp.dot(mixed_terms, matrix, precision=HIGH)

def orthogonalize(matrix):
    matrix = matrix / (jnp.sqrt(jnp.sum(matrix * matrix)) + EPS_FRAME)
    for sweep_number in range(5):
        gram_matrix = jnp.dot(matrix, matrix.T, precision=HIGH)
        matrix = newton_step(matrix, gram_matrix)
    return matrix

def latent_forward(params, inputs):
    ada, qkv, proj, upper, lower, bias_ada, bias_qkv, bias_out, bias_up, bias_down = params
    tokens, condition = inputs
    shifted = low(jax.nn.silu(condition))
    modulation = low_back(jnp.dot(shifted[None, :], ada, precision=HIGH))[0] + bias_ada
    shift_one, scale_one, gate_one, shift_two, scale_two, gate_two = jnp.split(modulation, 6)
    normed = low(layer_norm(tokens) * (1.0 + scale_one) + shift_one)
    packed = low(low_back(jnp.dot(normed, qkv, precision=HIGH)) + bias_qkv)
    query_heads = packed[:, :D].reshape(SEQ, HEADS, HEAD)
    key_heads = packed[:, D:2 * D].reshape(SEQ, HEADS, HEAD)
    value_heads = packed[:, 2 * D:].reshape(SEQ, HEADS, HEAD)
    scores = low_back(jnp.einsum('qhe,khe->hqk', query_heads, key_heads, precision=HIGH) * (1.0 / math.sqrt(HEAD)))
    soft_weights = low(jax.nn.softmax(scores, axis=-1))
    attended = jnp.einsum('hqk,khe->qhe', soft_weights, value_heads, precision=HIGH).reshape(SEQ, D)
    attended = low(low_back(attended))
    branch = low_back(jnp.dot(attended, proj, precision=HIGH)) + bias_out
    middle = tokens + gate_one * branch
    normed_two = low(layer_norm(middle) * (1.0 + scale_two) + shift_two)
    before = low_back(jnp.dot(normed_two, upper, precision=HIGH)) + bias_up
    hidden = low(jax.nn.gelu(before, approximate=True))
    result = low_back(jnp.dot(hidden, lower, precision=HIGH)) + bias_down
    return middle + gate_two * result

def block_forward(weights, biases, tokens, condition, live_slots):
    ada, qkv, proj, upper, lower = [low(matrix) for matrix in weights]
    bias_low = low(biases)
    bias_ada = bias_low[:6 * D]
    bias_query = bias_low[6 * D:7 * D]
    bias_value = bias_low[7 * D:8 * D]
    bias_out = bias_low[8 * D:9 * D]
    bias_up = bias_low[9 * D:9 * D + FF]
    bias_down = bias_low[9 * D + FF:]
    bias_qkv = jnp.concatenate([bias_query, jnp.zeros((D,), jnp.float32), bias_value])
    params = (ada, qkv, proj, upper, lower, bias_ada, bias_qkv, bias_out, bias_up, bias_down)

    def single(inputs):
        return latent_forward(params, inputs)
    outputs = lax.map(jax.checkpoint(single), (tokens, condition))
    return jnp.where(live_slots[:, None, None], outputs, 0.0)

def reference(tokens, cotangent, labels, timesteps, counts, class_table, time_table, ada_weight, qkv_weight, out_weight, up_weight, down_weight, biases, ada_moment, qkv_moment, out_moment, up_moment, down_moment, bias_moment):
    slot_ids = jnp.arange(SLOTS, dtype=jnp.int32)
    live_slots = slot_ids % LAT_DEV < counts[slot_ids // LAT_DEV]
    condition = class_table.astype(jnp.float32)[labels] + time_table.astype(jnp.float32)[timesteps]
    weights = (ada_weight, qkv_weight, out_weight, up_weight, down_weight)

    def wrapped(weight_list, bias_vector, inputs, conditions):
        return block_forward(weight_list, bias_vector, inputs, conditions, live_slots)
    output, pullback = jax.vjp(wrapped, weights, biases, tokens.astype(jnp.float32), condition)
    weight_grads, bias_grad, input_grad, cond_grad = pullback(cotangent.astype(jnp.float32))
    moments = (ada_moment, qkv_moment, out_moment, up_moment, down_moment)
    new_moments = [MOMENTUM * moment + grad for moment, grad in zip(moments, weight_grads)]
    new_weights = []
    for matrix, moment in zip(weights, new_moments):
        flipped = matrix.shape[0] > matrix.shape[1]
        frame = orthogonalize(moment.T if flipped else moment)
        frame = frame.T if flipped else frame
        factor = math.sqrt(max(matrix.shape) / matrix.shape[0])
        new_weights.append(matrix - STEP_RATE * factor * frame)
    bias_moment_new = MOMENTUM * bias_moment + bias_grad
    bias_new = biases - BIAS_RATE / math.sqrt(TOKENS) * bias_moment_new
    return (output.astype(jnp.bfloat16), input_grad, cond_grad, weight_grads[0], weight_grads[1], weight_grads[2], weight_grads[3], weight_grads[4], bias_grad, new_weights[0], new_weights[1], new_weights[2], new_weights[3], new_weights[4], bias_new, new_moments[0], new_moments[1], new_moments[2], new_moments[3], new_moments[4], bias_moment_new)
```

```python
import functools
import math

import jax
import jax.numpy as jnp
from jax import lax
from jax.experimental import pallas as pl
from jax.experimental.pallas import tpu as pltpu
from jax.sharding import PartitionSpec as P

D = 384
FF = 1536
HEAD = 64
N_FSDP = 16
N_Z = 4
BOTH = ("dp", "fsdp")

MOMENTUM = 0.95
STEP_RATE = 1.2
BIAS_RATE = 0.3
EPS_NORM = 1e-06
EPS_FRAME = 1e-07
COEF_A = 3.4445
COEF_B = -4.775
COEF_C = 2.0315
HIGH = lax.Precision.HIGHEST
F32 = jnp.float32
BF16 = jnp.bfloat16


def layer_norm_kept(vectors):
    centred = vectors - jnp.mean(vectors, axis=-1, keepdims=True)
    spread = jnp.mean(centred * centred, axis=-1, keepdims=True)
    inverse = lax.rsqrt(spread + EPS_NORM)
    return (centred * inverse, inverse)


def norm_backward(grad_normed, normed, inverse):
    centred_grad = grad_normed - jnp.mean(grad_normed, axis=-1, keepdims=True)
    return inverse * (
        centred_grad - normed * jnp.mean(grad_normed * normed, axis=-1, keepdims=True)
    )


def times_transposed(left_side, rows):
    return jnp.einsum("lsd,kd->lsk", left_side, rows, preferred_element_type=F32)


def times_rows(left_side, rows):
    return jnp.einsum("lsk,kd->lsd", left_side, rows, preferred_element_type=F32)


def weight_grad_rows(grads, inputs):
    return jnp.einsum("lsk,lsd->kd", grads, inputs, preferred_element_type=F32)


def swap_cores(block):
    return lax.ppermute(block, "dp", [(d, d ^ 1) for d in range(2 * N_Z)])


def shift_z(block, step):
    pairs = [(d, ((d // 2 + step) % N_Z) * 2 + d % 2) for d in range(2 * N_Z)]
    return lax.ppermute(block, "dp", pairs)


def pick(blocks, place, axis=0):
    return lax.dynamic_index_in_dim(blocks, place, axis, keepdims=False)


def gather_z(block, z_place):
    steps = [block] + [shift_z(block, step) for step in (1, 3, 2)]
    line = jnp.zeros((N_Z,) + block.shape, block.dtype)
    for step, piece in zip((0, 1, 3, 2), steps):
        line = lax.dynamic_update_index_in_dim(line, piece, (z_place - step) % N_Z, 0)
    return line


def join_cores(own, other, core_place, axis):
    first = jnp.where(core_place == 0, own, other)
    second = jnp.where(core_place == 0, other, own)
    return jnp.stack([first, second], axis=axis)


def exchange_fsdp(blocks):
    return lax.all_to_all(blocks, "fsdp", split_axis=0, concat_axis=0, tiled=True)


def split(value):
    high = value.astype(BF16)
    return high, (value - high.astype(F32)).astype(BF16)


def times_split(left, right):
    def dot(a, b):
        return jnp.dot(a, b, preferred_element_type=F32)

    return dot(left[0], right[0]) + (dot(left[0], right[1]) + dot(left[1], right[0]))


def newton_kernel(top_ref, bottom_ref, block_ref, out_ref):
    def times(left, right):
        return jnp.dot(left, right, precision=HIGH, preferred_element_type=F32)

    third = D // 3
    top = top_ref[...]
    bottom = bottom_ref[...]
    middle = bottom[:, third : 2 * third]
    gram = jnp.concatenate(
        [
            top,
            jnp.concatenate([top[:, third : 2 * third].T, bottom[:, :third], middle], axis=1),
            jnp.concatenate([top[:, 2 * third :].T, middle.T, bottom[:, 2 * third :]], axis=1),
        ],
        axis=0,
    )
    rows = lax.broadcasted_iota(jnp.int32, (D, D), 0)
    cols = lax.broadcasted_iota(jnp.int32, (D, D), 1)
    same = rows == cols
    square_sum = jnp.sum(jnp.where(same, gram, 0.0))
    scale = 1.0 / (jnp.sqrt(square_sum) + EPS_FRAME)
    gram = gram * scale * scale
    product = None
    for sweep in range(5):
        exact = sweep < 1
        gram_parts = None if exact else split(gram)
        squared = times(gram, gram) if exact else times_split(gram_parts, gram_parts)
        step = COEF_B * gram + COEF_C * squared + jnp.where(same, COEF_A, 0.0)
        step_parts = split(step)
        if product is None:
            product = step
        else:
            product = times_split(step_parts, split(product))
        if exact:
            gram = times(times(step, gram), step)
        elif sweep < 4:
            gram = times_split(split(times_split(step_parts, gram_parts)), step_parts)
    frames = times_split(split(block_ref[...]), split(product * scale))
    out_ref[...] = frames.astype(BF16)


def newton_frames(top, bottom, block):
    return pl.pallas_call(
        newton_kernel,
        out_shape=jax.ShapeDtypeStruct((D, D), BF16),
        compiler_params=pltpu.CompilerParams(vmem_limit_bytes=16 * 1024 * 1024),
        name="newton",
    )(top, bottom, block)


SEND_ROWS = 48


def repack_kernel(
    own_first, one_first, two_first, three_first, own_second, one_second, two_second, three_second,
    mods, out_ref, first, second, stage,
):
    def total(own, *others):
        value = own[...]
        for other in others:
            value = value + other[...].astype(F32)
        return value

    first[...] = total(own_first, one_first, two_first, three_first)
    second[...] = total(own_second, one_second, two_second, three_second)
    stage[...] = jnp.zeros_like(stage)
    for place in range(N_FSDP):
        stage[0:9, :] = first[9 * place : 9 * place + 9, :]
        stage[9:12, :] = second[3 * place : 3 * place + 3, :]
        stage[12:24, :] = second[48 + 12 * place : 60 + 12 * place, :]
        stage[24:36, :] = second[240 + 12 * place : 252 + 12 * place, :]
        stage[36:37, :] = first[144 + place : 145 + place, :]
        stage[37:38, :] = mods[place : place + 1, :]
        out_ref[place] = stage[...].astype(BF16)


def repack(first_terms, second_terms, mods):
    return pl.pallas_call(
        repack_kernel,
        out_shape=jax.ShapeDtypeStruct((N_FSDP, SEND_ROWS, D), BF16),
        scratch_shapes=[
            pltpu.VMEM((160, D), F32),
            pltpu.VMEM((432, D), F32),
            pltpu.VMEM((SEND_ROWS, D), F32),
        ],
        compiler_params=pltpu.CompilerParams(vmem_limit_bytes=8 * 1024 * 1024),
        name="repack",
    )(*first_terms, *second_terms, mods)


def prep_kernel(
    labels, timesteps, class_ref, time_ref, ada, qkv, out, up, down, bias,
    first_ref, second_ref, cond_ref, stage,
):
    def looked_up(places, table):
        shape = (8, table.shape[0])
        rows = lax.broadcasted_iota(jnp.int32, shape, 0)
        entry = lax.broadcasted_iota(jnp.int32, shape, 1)
        hot = jnp.where(rows == 0, places[0], places[1]) == entry
        return jnp.dot(hot.astype(F32).astype(BF16), table[...], preferred_element_type=F32)

    condition = (looked_up(labels, class_ref) + looked_up(timesteps, time_ref))[:2]
    cond_ref[...] = condition
    stage[...] = jnp.zeros_like(stage)
    stage[0:18, :] = ada[...]
    stage[18:27, :] = qkv[...]
    stage[27:28, : bias.shape[1]] = bias[...]
    stage[28:30, :] = jax.nn.silu(condition)
    stage[32:35, :] = out[...]
    stage[35:47, :] = up[...]
    stage[47:59, :] = down[...]
    low = stage[...].astype(BF16)
    for place in range(N_FSDP):
        first_ref[place] = low[:32]
    second_ref[...] = low[32:]


def prepare(labels, timesteps, class_table, time_table, weight_rows, biases):
    scalars = pl.BlockSpec(memory_space=pltpu.SMEM)
    arrays = (class_table, time_table, *weight_rows, biases[None])
    return pl.pallas_call(
        prep_kernel,
        grid=(1,),
        out_shape=(
            jax.ShapeDtypeStruct((N_FSDP, 32, D), BF16),
            jax.ShapeDtypeStruct((32, D), BF16),
            jax.ShapeDtypeStruct((2, D), F32),
        ),
        in_specs=[scalars, scalars]
        + [pl.BlockSpec(array.shape, lambda step: (0, 0)) for array in arrays],
        out_specs=(
            pl.BlockSpec((N_FSDP, 32, D), lambda step: (0, 0, 0)),
            pl.BlockSpec((32, D), lambda step: (0, 0)),
            pl.BlockSpec((2, D), lambda step: (0, 0)),
        ),
        scratch_shapes=[pltpu.VMEM((64, D), F32)],
        compiler_params=pltpu.CompilerParams(vmem_limit_bytes=60 * 1024 * 1024),
        name="prepare",
    )(labels, timesteps, *arrays)


ROWS = (18, 9, 3, 12, 12)


def moments_kernel(incoming, mods, cond, *refs):
    old = refs[:5]
    grads = refs[5:10]
    new = refs[10:15]
    bias_ref, owner_ref = refs[15:]
    total = incoming[0].astype(F32)
    for place in range(1, N_FSDP):
        total = total + incoming[place].astype(F32)
    grads[0][...] = jnp.dot(mods[...], cond[...], preferred_element_type=F32)
    grads[1][...] = total[0:9]
    grads[2][...] = total[9:12]
    grads[3][...] = total[12:24]
    grads[4][...] = total[24:36]
    bias_ref[...] = total[36:37]
    owner_ref[...] = jnp.zeros_like(owner_ref)
    for kind in range(5):
        value = MOMENTUM * old[kind][...] + grads[kind][...]
        new[kind][...] = value
        for owner in range(kind, N_FSDP, 5):
            owner_ref[owner, 0 : ROWS[kind], :] = value


def update_moments(incoming, mods, cond, moment_rows):
    shapes = [jax.ShapeDtypeStruct((count, D), F32) for count in ROWS]
    results = pl.pallas_call(
        moments_kernel,
        out_shape=(
            *shapes,
            *shapes,
            jax.ShapeDtypeStruct((1, D), F32),
            jax.ShapeDtypeStruct((N_FSDP, 24, D), F32),
        ),
        compiler_params=pltpu.CompilerParams(vmem_limit_bytes=16 * 1024 * 1024),
        name="moments",
    )(incoming, mods, cond, *moment_rows)
    return results[:5], results[5:10], results[10], results[11]


def finish_kernel(returned, *refs):
    factors = (math.sqrt(6.0), math.sqrt(3.0), 1.0, math.sqrt(FF / D), 1.0)
    for kind in range(5):
        frame = returned[kind].astype(F32)[: ROWS[kind]]
        refs[5 + kind][...] = refs[kind][...] - STEP_RATE * factors[kind] * frame


def finish_weights(returned, weight_rows):
    return pl.pallas_call(
        finish_kernel,
        out_shape=[jax.ShapeDtypeStruct((count, D), F32) for count in ROWS],
        compiler_params=pltpu.CompilerParams(vmem_limit_bytes=8 * 1024 * 1024),
        name="finish",
    )(returned, *weight_rows)


def attention_kernel(packed, attended):
    def dot(left, right, contract):
        return lax.dot_general(
            left, right, ((contract[:1], contract[1:]), ((), ())), preferred_element_type=F32
        )

    score_scale = 1.0 / math.sqrt(HEAD)
    lane = lax.broadcasted_iota(jnp.int32, (packed.shape[1], 2 * HEAD), 1)
    zero = jnp.zeros((), BF16)
    for pair in range(D // (2 * HEAD)):
        start = pair * 2 * HEAD
        query = packed[0, :, start : start + 2 * HEAD]
        key = packed[0, :, D + start : D + start + 2 * HEAD]
        value = packed[0, :, 2 * D + start : 2 * D + start + 2 * HEAD]
        mixed = None
        for head in range(2):
            own = (lane >= head * HEAD) & (lane < (head + 1) * HEAD)
            scores = dot(jnp.where(own, query, zero), key, (1, 1)) * score_scale
            exponent = jnp.exp(scores - jnp.max(scores, axis=-1, keepdims=True))
            probs = exponent * (1.0 / jnp.sum(exponent, axis=-1, keepdims=True))
            term = dot(probs.astype(BF16), jnp.where(own, value, zero), (1, 0))
            mixed = term if mixed is None else mixed + term
        attended[0, :, start : start + 2 * HEAD] = mixed.astype(BF16)


def attention(packed):
    slot_count, length, _ = packed.shape
    return pl.pallas_call(
        attention_kernel,
        grid=(slot_count,),
        out_shape=jax.ShapeDtypeStruct((slot_count, length, D), BF16),
        in_specs=[pl.BlockSpec((1, length, 3 * D), lambda place: (place, 0, 0))],
        out_specs=pl.BlockSpec((1, length, D), lambda place: (place, 0, 0)),
        compiler_params=pltpu.CompilerParams(vmem_limit_bytes=12 * 1024 * 1024),
        cost_estimate=pl.CostEstimate(
            flops=1_000_000_000, bytes_accessed=3_000_000, transcendentals=800_000
        ),
        name="attention",
    )(packed)


def attention_back_kernel(
    packed, branch_grad, out_rows, attn_in, qkv_rows, tokens, scale_one, middle_grad,
    qkv_grad, input_grad, shift_sum, scale_sum, query_sum, value_sum,
):
    def dot(left, right, contract):
        return lax.dot_general(
            left, right, ((contract[:1], contract[1:]), ((), ())), preferred_element_type=F32
        )

    score_scale = 1.0 / math.sqrt(HEAD)
    attended_grad = dot(branch_grad[0], out_rows[...], (1, 0)).astype(BF16)
    lane = lax.broadcasted_iota(jnp.int32, (attended_grad.shape[0], 2 * HEAD), 1)
    inside = attn_in[0]
    zero = jnp.zeros((), BF16)
    first_step = pl.program_id(0) == 0
    grad_inside = None
    for pair in range(D // (2 * HEAD)):
        start = pair * 2 * HEAD
        span = slice(start, start + 2 * HEAD)
        query = packed[0, :, start : start + 2 * HEAD]
        key = packed[0, :, D + start : D + start + 2 * HEAD]
        value = packed[0, :, 2 * D + start : 2 * D + start + 2 * HEAD]
        pair_grad = attended_grad[:, span]
        sums = [None, None, None]
        for head in range(2):
            own = (lane >= head * HEAD) & (lane < (head + 1) * HEAD)
            query_own = jnp.where(own, query, zero)
            key_own = jnp.where(own, key, zero)
            grad_own = jnp.where(own, pair_grad, zero)
            scores = dot(query_own, key, (1, 1)) * score_scale
            exponent = jnp.exp(scores - jnp.max(scores, axis=-1, keepdims=True))
            probs = exponent * (1.0 / jnp.sum(exponent, axis=-1, keepdims=True))
            grad_probs = dot(grad_own, value, (1, 1))
            grad_scores = probs * (
                grad_probs - jnp.sum(grad_probs * probs, axis=-1, keepdims=True)
            )
            low_scores = grad_scores.astype(BF16)
            terms = (
                dot(low_scores, key_own, (1, 0)),
                dot(low_scores, query_own, (0, 0)),
                dot(probs.astype(BF16), grad_own, (0, 0)),
            )
            sums = [term if old is None else old + term for old, term in zip(sums, terms)]
        grad_query = sums[0] * score_scale
        grad_key = sums[1] * score_scale
        query_sum[0, :, span] = jnp.sum(grad_query, axis=0, keepdims=True)
        value_sum[0, :, span] = jnp.sum(sums[2], axis=0, keepdims=True)
        for third, part in enumerate((grad_query, grad_key, sums[2])):
            part = part.astype(BF16)
            place = slice(third * D + start, third * D + start + 2 * HEAD)
            term = dot(part, inside, (0, 0))

            @pl.when(first_step)
            def _(place=place, term=term):
                qkv_grad[place, :] = term

            @pl.when(jnp.logical_not(first_step))
            def _(place=place, term=term):
                qkv_grad[place, :] += term

            back = dot(part, qkv_rows[place, :], (1, 0))
            grad_inside = back if grad_inside is None else grad_inside + back
    normed, inverse = layer_norm_kept(tokens[0].astype(F32))
    shift_sum[0] = jnp.sum(grad_inside, axis=0, keepdims=True)
    scale_sum[0] = jnp.sum(grad_inside * normed, axis=0, keepdims=True)
    input_grad[0] = middle_grad[0] + norm_backward(
        grad_inside * (1.0 + scale_one[0]), normed, inverse
    )


def attention_back(
    packed, branch_grad, out_rows, attn_in, qkv_rows, tokens, scale_one, middle_grad
):
    slot_count, length, _ = tokens.shape

    def latent(width, rows=length):
        return pl.BlockSpec((1, rows, width), lambda place: (place, 0, 0))

    def whole(rows):
        return pl.BlockSpec((rows, D), lambda place: (0, 0))

    small = jax.ShapeDtypeStruct((slot_count, 1, D), F32)
    return pl.pallas_call(
        attention_back_kernel,
        grid=(slot_count,),
        out_shape=(
            jax.ShapeDtypeStruct((3 * D, D), F32),
            jax.ShapeDtypeStruct(tokens.shape, F32),
            small,
            small,
            small,
            small,
        ),
        in_specs=[
            latent(3 * D), latent(D), whole(D), latent(D), whole(3 * D), latent(D), latent(D, 1),
            latent(D),
        ],
        out_specs=(whole(3 * D), latent(D)) + (latent(D, 1),) * 4,
        compiler_params=pltpu.CompilerParams(vmem_limit_bytes=28 * 1024 * 1024),
        cost_estimate=pl.CostEstimate(
            flops=3_500_000_000, bytes_accessed=8_000_000, transcendentals=800_000
        ),
        name="attention_back",
    )(packed, branch_grad, out_rows, attn_in, qkv_rows, tokens, scale_one, middle_grad)


def on_device(
    tokens,
    cotangent,
    labels,
    timesteps,
    counts,
    class_table,
    time_table,
    ada_weight,
    qkv_weight,
    out_weight,
    up_weight,
    down_weight,
    biases,
    ada_moment,
    qkv_moment,
    out_moment,
    up_moment,
    down_moment,
    bias_moment,
):
    slot_count, length, _ = tokens.shape
    dp_place = lax.axis_index("dp")
    z_place = dp_place // 2
    core_place = dp_place % 2
    live_slots = (jnp.arange(slot_count) < counts[0])[:, None, None]

    weight_rows = [
        ada_weight.T,
        qkv_weight.T,
        out_weight.T,
        up_weight.T,
        down_weight,
    ]
    bias_shard = biases.shape[0]
    first_sent, second_shard, condition = prepare(
        labels, timesteps, class_table, time_table, weight_rows, biases
    )
    cond_act, silu_back = jax.vjp(jax.nn.silu, condition)
    cond_low = cond_act.astype(BF16)
    first_near = exchange_fsdp(first_sent)

    def cut(start, count):
        return first_near[:, start : start + count].reshape(N_FSDP * count, D)

    first_block = jnp.concatenate([cut(0, 18), cut(18, 9), cut(27, 1), cut(28, 2)], axis=0)
    second_near = gather_z(second_shard, z_place).reshape(1, N_Z * 32, D)
    second_near = exchange_fsdp(jnp.broadcast_to(second_near, (N_FSDP, N_Z * 32, D)))
    second_near = second_near.reshape(N_FSDP, N_Z, 32, D)

    def cut_line(start, count):
        rows = second_near[:, :, start : start + count].transpose(1, 0, 2, 3)
        return rows.reshape(N_Z, N_FSDP * count, D)

    first_line = gather_z(first_block, z_place)
    first_full = join_cores(first_line, swap_cores(first_line), core_place, 1)
    second_line = jnp.concatenate([cut_line(0, 3), cut_line(3, 12), cut_line(15, 12)], axis=1)

    def rows_of(full, start, count):
        return full[:, :, start : start + count].reshape(2 * N_Z * count, D)

    ada_rows = rows_of(first_full, 0, 288)
    qkv_rows = rows_of(first_full, 288, 144)
    bias_wide = rows_of(first_full, 432, 16)[:, :bias_shard].reshape(-1).astype(F32)
    cond_all = (
        first_full[:, :, 448:480]
        .reshape(N_Z, 2, N_FSDP, slot_count, D)
        .transpose(2, 0, 1, 3, 4)
        .reshape(-1, D)
    )
    bias_ada = bias_wide[: 6 * D]
    bias_query = bias_wide[6 * D : 7 * D]
    bias_value = bias_wide[7 * D : 8 * D]
    bias_out = bias_wide[8 * D : 9 * D]
    bias_up = bias_wide[9 * D : 9 * D + FF]
    bias_down = bias_wide[9 * D + FF :]

    modulation = jnp.einsum("ld,kd->lk", cond_low, ada_rows, preferred_element_type=F32) + bias_ada
    pieces = jnp.split(modulation[:, None, :], 6, axis=2)
    shift_one, scale_one, gate_one, shift_two, scale_two, gate_two = pieces
    inputs = tokens.astype(F32)
    normed_one, _ = layer_norm_kept(inputs)
    attn_in = (normed_one * (1.0 + scale_one) + shift_one).astype(BF16)
    qkv_bias = jnp.concatenate([bias_query, jnp.zeros_like(bias_query), bias_value])
    packed = (times_transposed(attn_in, qkv_rows) + qkv_bias).astype(BF16)
    attended, second_line = lax.optimization_barrier((attention(packed), second_line))
    second_other = swap_cores(second_line)
    second_full = join_cores(second_line, second_other, core_place, 1)
    out_rows = rows_of(second_full, 0, 48)
    up_rows = rows_of(second_full, 48, 192)
    down_rows = rows_of(second_full, 240, 192)
    branch = times_transposed(attended, out_rows) + bias_out
    middle = inputs + gate_one * branch
    normed_two, inverse_two = layer_norm_kept(middle)
    mlp_in = (normed_two * (1.0 + scale_two) + shift_two).astype(BF16)
    before = times_transposed(mlp_in, up_rows) + bias_up
    activated, gelu_back = jax.vjp(functools.partial(jax.nn.gelu, approximate=True), before)
    hidden = activated.astype(BF16)
    result = times_rows(hidden, down_rows) + bias_down
    output = jnp.where(live_slots, middle + gate_two * result, 0.0).astype(BF16)

    grad_out = jnp.where(live_slots, cotangent.astype(F32), 0.0)
    grad_result = grad_out * gate_two
    grad_gate_two = jnp.sum(grad_out * result, axis=1)
    grad_result_low = grad_result.astype(BF16)
    local_down = weight_grad_rows(hidden, grad_result_low)
    grad_hidden = times_transposed(grad_result_low, down_rows)
    grad_before = gelu_back(grad_hidden)[0]
    grad_before_low = grad_before.astype(BF16)
    local_up = weight_grad_rows(grad_before_low, mlp_in)
    grad_mlp_in = times_rows(grad_before_low, up_rows)
    grad_shift_two = jnp.sum(grad_mlp_in, axis=1)
    grad_scale_two = jnp.sum(grad_mlp_in * normed_two, axis=1)
    grad_middle = grad_out + norm_backward(grad_mlp_in * (1.0 + scale_two), normed_two, inverse_two)
    grad_branch = grad_middle * gate_one
    grad_gate_one = jnp.sum(grad_middle * branch, axis=1)
    grad_branch_low = grad_branch.astype(BF16)
    local_out = weight_grad_rows(grad_branch_low, attended)

    def by_dp(rows):
        return rows.reshape(N_Z, 2, -1, D)

    second_terms = [by_dp(local_out), by_dp(local_up), by_dp(local_down)]
    second_leaving = jnp.concatenate(
        [pick(terms, 1 - core_place, 1).astype(BF16) for terms in second_terms], axis=1
    )
    grad_branch_low, second_leaving = lax.optimization_barrier((grad_branch_low, second_leaving))
    second_arrived = swap_cores(second_leaving)

    local_qkv, input_grad, shift_sum, scale_sum, query_sum, value_sum = attention_back(
        packed, grad_branch_low, out_rows, attn_in, qkv_rows, tokens, scale_one, grad_middle
    )
    local_qkv, second_arrived = lax.optimization_barrier((local_qkv, second_arrived))
    second_own = jnp.concatenate([pick(terms, core_place, 1) for terms in second_terms], axis=1)
    second_line_sum = second_own + second_arrived.astype(F32)
    second_pieces = [
        shift_z(pick(second_line_sum, (z_place + step) % N_Z).astype(BF16), step)
        for step in (1, 3, 2)
    ]
    grad_shift_one = shift_sum[:, 0]
    grad_scale_one = scale_sum[:, 0]
    grad_mod = jnp.concatenate(
        [
            grad_shift_one,
            grad_scale_one,
            grad_gate_one,
            grad_shift_two,
            grad_scale_two,
            grad_gate_two,
        ],
        axis=1,
    )
    grad_mod_low = grad_mod.astype(BF16)
    token_axes = (0, 1)
    local_bias = jnp.concatenate(
        [
            jnp.sum(grad_mod, axis=0).reshape(6, D),
            jnp.sum(query_sum, axis=token_axes)[None],
            jnp.sum(value_sum, axis=token_axes)[None],
            jnp.sum(grad_branch, axis=token_axes)[None],
            jnp.sum(grad_before, axis=token_axes).reshape(FF // D, D),
            jnp.sum(grad_result, axis=token_axes)[None],
        ]
    )
    bias_terms = jnp.pad(
        local_bias.reshape(N_Z, 2, N_FSDP, bias_shard), ((0, 0),) * 3 + ((0, D - bias_shard),)
    )

    mod_rows = jnp.pad(
        grad_mod_low.reshape(slot_count, N_Z, 2, 288).transpose(1, 2, 0, 3),
        ((0, 0),) * 3 + ((0, D - 288),),
    )
    first_terms = jnp.concatenate([by_dp(local_qkv), bias_terms], axis=2)
    count_first = first_terms.shape[2]
    leaving = jnp.concatenate(
        [pick(first_terms, 1 - core_place, 1).astype(BF16), pick(mod_rows, 1 - core_place, 1)],
        axis=1,
    )
    leaving, *second_pieces = lax.optimization_barrier((leaving, *second_pieces))
    arrived = swap_cores(leaving)
    line_terms = pick(first_terms, core_place, 1) + arrived[:, :count_first].astype(F32)
    line_mod = join_cores(
        pick(mod_rows, core_place, 1), arrived[:, count_first:], core_place, 1
    ).reshape(N_Z, 2 * slot_count, D)
    line = jnp.concatenate([line_terms.astype(BF16), line_mod], axis=1)
    mods = jnp.zeros((N_Z, 2 * slot_count, 288), BF16)
    mods = lax.dynamic_update_index_in_dim(mods, pick(line_mod, z_place)[:, :288], z_place, 0)
    first_pieces = []
    for step in (1, 3, 2):
        piece = shift_z(pick(line, (z_place + step) % N_Z), step)
        first_pieces.append(piece[:count_first])
        mods = lax.dynamic_update_index_in_dim(
            mods, piece[count_first:, :288], (z_place - step) % N_Z, 0
        )
    lat_dp = 2 * N_Z * slot_count
    mod_by_shard = mods.astype(F32).reshape(lat_dp, N_FSDP, 18).transpose(1, 0, 2)
    mod_by_shard = jnp.pad(mod_by_shard.reshape(N_FSDP, 288), ((0, 0), (0, D - 288)))
    outgoing = repack(
        [pick(line_terms, z_place), *first_pieces],
        [pick(second_line_sum, z_place), *second_pieces],
        mod_by_shard,
    )
    incoming = exchange_fsdp(outgoing)
    mod_all = incoming[:, 37, :288].reshape(N_FSDP * lat_dp, 18).T
    moment_rows = [ada_moment.T, qkv_moment.T, out_moment.T, up_moment.T, down_moment]
    grad_rows, new_moments, bias_row, to_owner = update_moments(
        incoming, mod_all, cond_all, moment_rows
    )
    bias_grad = bias_row[0, :bias_shard]
    block = exchange_fsdp(to_owner).reshape(N_FSDP * 24, D)
    gram = jnp.einsum("nk,nd->kd", block, block, precision=HIGH)
    third = D // 3
    top = gram[:third]
    bottom = jnp.concatenate(
        [
            gram[third : 2 * third, third : 2 * third],
            gram[third : 2 * third, 2 * third :],
            gram[2 * third :, 2 * third :],
        ],
        axis=1,
    )
    half = jnp.where(core_place == 0, top, bottom)
    half = half + swap_cores(jnp.where(core_place == 0, bottom, top))
    half = half + shift_z(half, 1) + shift_z(half, 3) + shift_z(half, 2)
    other_half = swap_cores(half)
    frames = newton_frames(
        jnp.where(core_place == 0, half, other_half),
        jnp.where(core_place == 0, other_half, half),
        block,
    )
    returned = exchange_fsdp(frames.reshape(N_FSDP, 24, D))

    new_rows = finish_weights(returned, weight_rows)

    grad_cond_act = jnp.dot(grad_mod_low, ada_rows, preferred_element_type=F32)
    cond_grad = silu_back(grad_cond_act)[0]
    bias_moment_new = MOMENTUM * bias_moment + bias_grad
    tokens_all = lax.axis_size(BOTH) * slot_count * length
    bias_new = biases - BIAS_RATE / math.sqrt(tokens_all) * bias_moment_new

    def columns(rows):
        return [rows[0].T, rows[1].T, rows[2].T, rows[3].T, rows[4]]

    return (
        output,
        input_grad,
        cond_grad,
        *columns(grad_rows),
        bias_grad,
        *columns(new_rows),
        bias_new,
        *columns(new_moments),
        bias_moment_new,
    )


def solution(mesh):
    latents = P(BOTH, None, None)
    vector = P(BOTH)
    column = P(None, BOTH)
    row = P(BOTH, None)
    matrices = (column, column, column, column, row)
    return jax.shard_map(
        on_device,
        mesh=mesh,
        in_specs=(
            latents,
            latents,
            vector,
            vector,
            vector,
            P(),
            P(),
            *matrices,
            vector,
            *matrices,
            vector,
        ),
        out_specs=(
            latents,
            latents,
            row,
            *matrices,
            vector,
            *matrices,
            vector,
            *matrices,
            vector,
        ),
        check_vma=False,
    )
```

```python
import functools
import math

import jax
import jax.numpy as jnp
from jax import lax
from jax.experimental import pallas as pl
from jax.experimental.pallas import tpu as pltpu
from jax.sharding import PartitionSpec as P

D = 384
FF = 1536
HEAD = 64
N_FSDP = 16
N_Z = 4
BOTH = ("dp", "fsdp")

MOMENTUM = 0.95
STEP_RATE = 1.2
BIAS_RATE = 0.3
EPS_NORM = 1e-06
EPS_FRAME = 1e-07
COEF_A = 3.4445
COEF_B = -4.775
COEF_C = 2.0315
HIGH = lax.Precision.HIGHEST
F32 = jnp.float32
BF16 = jnp.bfloat16


def layer_norm_kept(vectors):
    centred = vectors - jnp.mean(vectors, axis=-1, keepdims=True)
    spread = jnp.mean(centred * centred, axis=-1, keepdims=True)
    inverse = lax.rsqrt(spread + EPS_NORM)
    return (centred * inverse, inverse)


def norm_backward(grad_normed, normed, inverse):
    centred_grad = grad_normed - jnp.mean(grad_normed, axis=-1, keepdims=True)
    return inverse * (
        centred_grad - normed * jnp.mean(grad_normed * normed, axis=-1, keepdims=True)
    )


def times_transposed(left_side, rows):
    return jnp.einsum("lsd,kd->lsk", left_side, rows, preferred_element_type=F32)


def times_rows(left_side, rows):
    return jnp.einsum("lsk,kd->lsd", left_side, rows, preferred_element_type=F32)


def weight_grad_rows(grads, inputs):
    return jnp.einsum("lsk,lsd->kd", grads, inputs, preferred_element_type=F32)


def swap_cores(block):
    return lax.ppermute(block, "dp", [(d, d ^ 1) for d in range(2 * N_Z)])


def shift_z(block, step):
    pairs = [(d, ((d // 2 + step) % N_Z) * 2 + d % 2) for d in range(2 * N_Z)]
    return lax.ppermute(block, "dp", pairs)


def pick(blocks, place, axis=0):
    return lax.dynamic_index_in_dim(blocks, place, axis, keepdims=False)


def gather_z(block, z_place):
    steps = [block] + [shift_z(block, step) for step in (1, 3, 2)]
    line = jnp.zeros((N_Z,) + block.shape, block.dtype)
    for step, piece in zip((0, 1, 3, 2), steps):
        line = lax.dynamic_update_index_in_dim(line, piece, (z_place - step) % N_Z, 0)
    return line


def join_cores(own, other, core_place, axis):
    first = jnp.where(core_place == 0, own, other)
    second = jnp.where(core_place == 0, other, own)
    return jnp.stack([first, second], axis=axis)


def exchange_fsdp(blocks):
    return lax.all_to_all(blocks, "fsdp", split_axis=0, concat_axis=0, tiled=True)


def split(value):
    high = value.astype(BF16)
    return high, (value - high.astype(F32)).astype(BF16)


def times_split(left, right):
    def dot(a, b):
        return jnp.dot(a, b, preferred_element_type=F32)

    return dot(left[0], right[0]) + (dot(left[0], right[1]) + dot(left[1], right[0]))


def newton_kernel(top_ref, bottom_ref, block_ref, out_ref):
    def times(left, right):
        return jnp.dot(left, right, precision=HIGH, preferred_element_type=F32)

    third = D // 3
    top = top_ref[...]
    bottom = bottom_ref[...]
    middle = bottom[:, third : 2 * third]
    gram = jnp.concatenate(
        [
            top,
            jnp.concatenate([top[:, third : 2 * third].T, bottom[:, :third], middle], axis=1),
            jnp.concatenate([top[:, 2 * third :].T, middle.T, bottom[:, 2 * third :]], axis=1),
        ],
        axis=0,
    )
    rows = lax.broadcasted_iota(jnp.int32, (D, D), 0)
    cols = lax.broadcasted_iota(jnp.int32, (D, D), 1)
    same = rows == cols
    square_sum = jnp.sum(jnp.where(same, gram, 0.0))
    scale = 1.0 / (jnp.sqrt(square_sum) + EPS_FRAME)
    gram = gram * scale * scale
    product = None
    for sweep in range(5):
        exact = sweep < 1
        gram_parts = None if exact else split(gram)
        squared = times(gram, gram) if exact else times_split(gram_parts, gram_parts)
        step = COEF_B * gram + COEF_C * squared + jnp.where(same, COEF_A, 0.0)
        step_parts = split(step)
        if product is None:
            product = step
        else:
            product = times_split(step_parts, split(product))
        if exact:
            gram = times(times(step, gram), step)
        elif sweep < 4:
            gram = times_split(split(times_split(step_parts, gram_parts)), step_parts)
    frames = times_split(split(block_ref[...]), split(product * scale))
    out_ref[...] = frames.astype(BF16)


def newton_frames(top, bottom, block):
    return pl.pallas_call(
        newton_kernel,
        out_shape=jax.ShapeDtypeStruct((D, D), BF16),
        compiler_params=pltpu.CompilerParams(vmem_limit_bytes=16 * 1024 * 1024),
        name="newton",
    )(top, bottom, block)


SEND_ROWS = 48


def repack_kernel(
    own_first, one_first, two_first, three_first, own_second, one_second, two_second, three_second,
    mods, out_ref, first, second, stage,
):
    def total(own, *others):
        value = own[...]
        for other in others:
            value = value + other[...].astype(F32)
        return value

    first[...] = total(own_first, one_first, two_first, three_first)
    second[...] = total(own_second, one_second, two_second, three_second)
    stage[...] = jnp.zeros_like(stage)
    for place in range(N_FSDP):
        stage[0:9, :] = first[9 * place : 9 * place + 9, :]
        stage[9:12, :] = second[3 * place : 3 * place + 3, :]
        stage[12:24, :] = second[48 + 12 * place : 60 + 12 * place, :]
        stage[24:36, :] = second[240 + 12 * place : 252 + 12 * place, :]
        stage[36:37, :] = first[144 + place : 145 + place, :]
        stage[37:38, :] = mods[place : place + 1, :]
        out_ref[place] = stage[...].astype(BF16)


def repack(first_terms, second_terms, mods):
    return pl.pallas_call(
        repack_kernel,
        out_shape=jax.ShapeDtypeStruct((N_FSDP, SEND_ROWS, D), BF16),
        scratch_shapes=[
            pltpu.VMEM((160, D), F32),
            pltpu.VMEM((432, D), F32),
            pltpu.VMEM((SEND_ROWS, D), F32),
        ],
        compiler_params=pltpu.CompilerParams(vmem_limit_bytes=8 * 1024 * 1024),
        name="repack",
    )(*first_terms, *second_terms, mods)


def prep_kernel(
    labels, timesteps, class_ref, time_ref, ada, qkv, out, up, down, bias,
    first_ref, second_ref, cond_ref, stage,
):
    def looked_up(places, table):
        shape = (8, table.shape[0])
        rows = lax.broadcasted_iota(jnp.int32, shape, 0)
        entry = lax.broadcasted_iota(jnp.int32, shape, 1)
        hot = jnp.where(rows == 0, places[0], places[1]) == entry
        return jnp.dot(hot.astype(F32).astype(BF16), table[...], preferred_element_type=F32)

    condition = (looked_up(labels, class_ref) + looked_up(timesteps, time_ref))[:2]
    cond_ref[...] = condition
    stage[...] = jnp.zeros_like(stage)
    stage[0:18, :] = ada[...]
    stage[18:27, :] = qkv[...]
    stage[27:28, : bias.shape[1]] = bias[...]
    stage[28:30, :] = jax.nn.silu(condition)
    stage[32:35, :] = out[...]
    stage[35:47, :] = up[...]
    stage[47:59, :] = down[...]
    low = stage[...].astype(BF16)
    for place in range(N_FSDP):
        first_ref[place] = low[:32]
    second_ref[...] = low[32:]


def prepare(labels, timesteps, class_table, time_table, weight_rows, biases):
    scalars = pl.BlockSpec(memory_space=pltpu.SMEM)
    arrays = (class_table, time_table, *weight_rows, biases[None])
    return pl.pallas_call(
        prep_kernel,
        grid=(1,),
        out_shape=(
            jax.ShapeDtypeStruct((N_FSDP, 32, D), BF16),
            jax.ShapeDtypeStruct((32, D), BF16),
            jax.ShapeDtypeStruct((2, D), F32),
        ),
        in_specs=[scalars, scalars]
        + [pl.BlockSpec(array.shape, lambda step: (0, 0)) for array in arrays],
        out_specs=(
            pl.BlockSpec((N_FSDP, 32, D), lambda step: (0, 0, 0)),
            pl.BlockSpec((32, D), lambda step: (0, 0)),
            pl.BlockSpec((2, D), lambda step: (0, 0)),
        ),
        scratch_shapes=[pltpu.VMEM((64, D), F32)],
        compiler_params=pltpu.CompilerParams(vmem_limit_bytes=60 * 1024 * 1024),
        name="prepare",
    )(labels, timesteps, *arrays)


ROWS = (18, 9, 3, 12, 12)


def moments_kernel(incoming, mods, cond, *refs):
    old = refs[:5]
    grads = refs[5:10]
    new = refs[10:15]
    bias_ref, owner_ref = refs[15:]
    total = incoming[0].astype(F32)
    for place in range(1, N_FSDP):
        total = total + incoming[place].astype(F32)
    grads[0][...] = jnp.dot(mods[...], cond[...], preferred_element_type=F32)
    grads[1][...] = total[0:9]
    grads[2][...] = total[9:12]
    grads[3][...] = total[12:24]
    grads[4][...] = total[24:36]
    bias_ref[...] = total[36:37]
    owner_ref[...] = jnp.zeros_like(owner_ref)
    for kind in range(5):
        value = MOMENTUM * old[kind][...] + grads[kind][...]
        new[kind][...] = value
        for owner in range(kind, N_FSDP, 5):
            owner_ref[owner, 0 : ROWS[kind], :] = value


def update_moments(incoming, mods, cond, moment_rows):
    shapes = [jax.ShapeDtypeStruct((count, D), F32) for count in ROWS]
    results = pl.pallas_call(
        moments_kernel,
        out_shape=(
            *shapes,
            *shapes,
            jax.ShapeDtypeStruct((1, D), F32),
            jax.ShapeDtypeStruct((N_FSDP, 24, D), F32),
        ),
        compiler_params=pltpu.CompilerParams(vmem_limit_bytes=16 * 1024 * 1024),
        name="moments",
    )(incoming, mods, cond, *moment_rows)
    return results[:5], results[5:10], results[10], results[11]


def finish_kernel(returned, *refs):
    factors = (math.sqrt(6.0), math.sqrt(3.0), 1.0, math.sqrt(FF / D), 1.0)
    for kind in range(5):
        frame = returned[kind].astype(F32)[: ROWS[kind]]
        refs[5 + kind][...] = refs[kind][...] - STEP_RATE * factors[kind] * frame


def finish_weights(returned, weight_rows):
    return pl.pallas_call(
        finish_kernel,
        out_shape=[jax.ShapeDtypeStruct((count, D), F32) for count in ROWS],
        compiler_params=pltpu.CompilerParams(vmem_limit_bytes=8 * 1024 * 1024),
        name="finish",
    )(returned, *weight_rows)


def attention_kernel(packed, attended):
    def dot(left, right, contract):
        return lax.dot_general(
            left, right, ((contract[:1], contract[1:]), ((), ())), preferred_element_type=F32
        )

    score_scale = 1.0 / math.sqrt(HEAD)
    lane = lax.broadcasted_iota(jnp.int32, (packed.shape[1], 2 * HEAD), 1)
    zero = jnp.zeros((), BF16)
    for pair in range(D // (2 * HEAD)):
        start = pair * 2 * HEAD
        query = packed[0, :, start : start + 2 * HEAD]
        key = packed[0, :, D + start : D + start + 2 * HEAD]
        value = packed[0, :, 2 * D + start : 2 * D + start + 2 * HEAD]
        mixed = None
        for head in range(2):
            own = (lane >= head * HEAD) & (lane < (head + 1) * HEAD)
            scores = dot(jnp.where(own, query, zero), key, (1, 1)) * score_scale
            exponent = jnp.exp(scores - jnp.max(scores, axis=-1, keepdims=True))
            probs = exponent * (1.0 / jnp.sum(exponent, axis=-1, keepdims=True))
            term = dot(probs.astype(BF16), jnp.where(own, value, zero), (1, 0))
            mixed = term if mixed is None else mixed + term
        attended[0, :, start : start + 2 * HEAD] = mixed.astype(BF16)


def attention(packed):
    slot_count, length, _ = packed.shape
    return pl.pallas_call(
        attention_kernel,
        grid=(slot_count,),
        out_shape=jax.ShapeDtypeStruct((slot_count, length, D), BF16),
        in_specs=[pl.BlockSpec((1, length, 3 * D), lambda place: (place, 0, 0))],
        out_specs=pl.BlockSpec((1, length, D), lambda place: (place, 0, 0)),
        compiler_params=pltpu.CompilerParams(vmem_limit_bytes=12 * 1024 * 1024),
        cost_estimate=pl.CostEstimate(
            flops=1_000_000_000, bytes_accessed=3_000_000, transcendentals=800_000
        ),
        name="attention",
    )(packed)


def attention_back_kernel(
    packed, branch_grad, out_rows, attn_in, qkv_rows, tokens, scale_one, middle_grad, *refs
):
    earlier = refs[0] if len(refs) == 8 else None
    qkv_grad, input_grad, shift_sum, scale_sum, query_sum, value_sum = refs[-6:]

    def dot(left, right, contract):
        return lax.dot_general(
            left, right, ((contract[:1], contract[1:]), ((), ())), preferred_element_type=F32
        )

    score_scale = 1.0 / math.sqrt(HEAD)
    attended_grad = dot(branch_grad[0], out_rows[...], (1, 0)).astype(BF16)
    lane = lax.broadcasted_iota(jnp.int32, (attended_grad.shape[0], 2 * HEAD), 1)
    inside = attn_in[0]
    zero = jnp.zeros((), BF16)
    grad_inside = None
    for pair in range(D // (2 * HEAD)):
        start = pair * 2 * HEAD
        span = slice(start, start + 2 * HEAD)
        query = packed[0, :, start : start + 2 * HEAD]
        key = packed[0, :, D + start : D + start + 2 * HEAD]
        value = packed[0, :, 2 * D + start : 2 * D + start + 2 * HEAD]
        pair_grad = attended_grad[:, span]
        sums = [None, None, None]
        for head in range(2):
            own = (lane >= head * HEAD) & (lane < (head + 1) * HEAD)
            query_own = jnp.where(own, query, zero)
            key_own = jnp.where(own, key, zero)
            grad_own = jnp.where(own, pair_grad, zero)
            scores = dot(query_own, key, (1, 1)) * score_scale
            exponent = jnp.exp(scores - jnp.max(scores, axis=-1, keepdims=True))
            probs = exponent * (1.0 / jnp.sum(exponent, axis=-1, keepdims=True))
            grad_probs = dot(grad_own, value, (1, 1))
            grad_scores = probs * (
                grad_probs - jnp.sum(grad_probs * probs, axis=-1, keepdims=True)
            )
            low_scores = grad_scores.astype(BF16)
            terms = (
                dot(low_scores, key_own, (1, 0)),
                dot(low_scores, query_own, (0, 0)),
                dot(probs.astype(BF16), grad_own, (0, 0)),
            )
            sums = [term if old is None else old + term for old, term in zip(sums, terms)]
        grad_query = sums[0] * score_scale
        grad_key = sums[1] * score_scale
        query_sum[0, :, span] = jnp.sum(grad_query, axis=0, keepdims=True)
        value_sum[0, :, span] = jnp.sum(sums[2], axis=0, keepdims=True)
        for third, part in enumerate((grad_query, grad_key, sums[2])):
            part = part.astype(BF16)
            place = slice(third * D + start, third * D + start + 2 * HEAD)
            term = dot(part, inside, (0, 0))
            qkv_grad[place, :] = term if earlier is None else earlier[place, :] + term
            back = dot(part, qkv_rows[place, :], (1, 0))
            grad_inside = back if grad_inside is None else grad_inside + back
    normed, inverse = layer_norm_kept(tokens[0].astype(F32))
    shift_sum[0] = jnp.sum(grad_inside, axis=0, keepdims=True)
    scale_sum[0] = jnp.sum(grad_inside * normed, axis=0, keepdims=True)
    input_grad[0] = middle_grad[0] + norm_backward(
        grad_inside * (1.0 + scale_one[0]), normed, inverse
    )


def attention_back(
    which, packed, branch_grad, out_rows, attn_in, qkv_rows, tokens, scale_one, middle_grad,
    earlier=(),
):
    _, length, _ = tokens.shape

    def latent(width, rows=length):
        return pl.BlockSpec((1, rows, width), lambda step: (which, 0, 0))

    def whole(rows):
        return pl.BlockSpec((rows, D), lambda step: (0, 0))

    one = pl.BlockSpec((1, 1, D), lambda step: (0, 0, 0))
    small = jax.ShapeDtypeStruct((1, 1, D), F32)
    return pl.pallas_call(
        attention_back_kernel,
        grid=(1,),
        out_shape=(
            jax.ShapeDtypeStruct((3 * D, D), F32),
            jax.ShapeDtypeStruct(tokens.shape, F32),
            small,
            small,
            small,
            small,
        ),
        in_specs=[
            latent(3 * D), latent(D), whole(D), latent(D), whole(3 * D), latent(D), latent(D, 1),
            latent(D),
        ]
        + ([whole(3 * D), pl.BlockSpec(memory_space=pl.ANY)] if earlier else []),
        out_specs=(whole(3 * D), latent(D), one, one, one, one),
        input_output_aliases={9: 1} if earlier else {},
        compiler_params=pltpu.CompilerParams(vmem_limit_bytes=60 * 1024 * 1024),
        cost_estimate=pl.CostEstimate(
            flops=1_800_000_000, bytes_accessed=5_000_000, transcendentals=400_000
        ),
        name="attention_back",
    )(packed, branch_grad, out_rows, attn_in, qkv_rows, tokens, scale_one, middle_grad, *earlier)


def mlp_kernel(
    place, attended, tokens, cotangent, mods, biases, own_line, other_line,
    output, middle_grad, branch_grad, sums, up_sum, leaving, own_terms,
    out_rows, out_w, up_w, down_w, hidden, slope, out_g, up_g, down_g,
):
    def dot(left, right, contract):
        return lax.dot_general(
            left, right, ((contract[:1], contract[1:]), ((), ())), preferred_element_type=F32
        )

    latent = pl.program_id(0)
    core = place[0]
    parts = ((out_w, out_g, 0, 48), (up_w, up_g, 48, 192), (down_w, down_g, 240, 192))

    @pl.when(latent == 0)
    def _():
        for weight, grad, start, count in parts:
            for z in range(N_Z):
                for line, side in ((own_line, core), (other_line, 1 - core)):
                    row = pl.multiple_of((2 * z + side) * count, 16)
                    weight[pl.ds(row, count), :] = line[z, start : start + count]
            grad[...] = jnp.zeros_like(grad)
        out_rows[...] = out_w[...]

    shift_two, scale_two, gate_one, gate_two = [
        mods[0, :, part * D : (part + 1) * D] for part in (3, 4, 2, 5)
    ]
    bias_out = biases[:, 8 * D : 9 * D]
    bias_up = biases[:, 9 * D : 9 * D + FF]
    bias_down = biases[:, 9 * D + FF :]
    attended_low = attended[0]
    branch = dot(attended_low, out_w[...], (1, 1)) + bias_out
    middle = tokens[0].astype(F32) + gate_one * branch
    normed, inverse = layer_norm_kept(middle)
    mlp_in = (normed * (1.0 + scale_two) + shift_two).astype(BF16)
    chunk = 512
    result = bias_down
    for start in range(0, FF, chunk):
        span = slice(start, start + chunk)
        before = dot(mlp_in, up_w[span, :], (1, 1)) + bias_up[:, span]
        square = before * before
        slant = math.sqrt(2.0 / math.pi)
        bend = jnp.tanh(before * (slant + slant * 0.044715 * square))
        share = 0.5 + 0.5 * bend
        low = (before * share).astype(BF16)
        hidden[:, span] = low
        slope[:, span] = share + before * (0.5 - 0.5 * bend * bend) * (
            slant + 3.0 * slant * 0.044715 * square
        )
        result = result + dot(low, down_w[span, :], (1, 0))
    live = latent < place[1]
    output[0] = jnp.where(live, middle + gate_two * result, 0.0).astype(BF16)
    grad_out = jnp.where(live, cotangent[0].astype(F32), 0.0)
    grad_result = grad_out * gate_two
    result_low = grad_result.astype(BF16)
    grad_in = None
    for start in range(0, FF, chunk):
        span = slice(start, start + chunk)
        down_g[span, :] += dot(hidden[:, span], result_low, (0, 0))
        grad_before = dot(result_low, down_w[span, :], (1, 1)) * slope[:, span]
        up_sum[0, :, span] = jnp.sum(grad_before, axis=0, keepdims=True)
        low = grad_before.astype(BF16)
        up_g[span, :] += dot(low, mlp_in, (0, 0))
        back = dot(low, up_w[span, :], (1, 0))
        grad_in = back if grad_in is None else grad_in + back
    grad_middle = grad_out + norm_backward(grad_in * (1.0 + scale_two), normed, inverse)
    grad_branch = grad_middle * gate_one
    branch_low = grad_branch.astype(BF16)
    out_g[...] += dot(branch_low, attended_low, (0, 0))
    middle_grad[0] = grad_middle
    branch_grad[0] = branch_low
    totals = (
        grad_middle * branch, grad_in, grad_in * normed, grad_out * result, grad_branch, grad_result,
    )
    for row, terms in enumerate(totals):
        sums[0, row : row + 1, :] = jnp.sum(terms, axis=0, keepdims=True)

    @pl.when(latent == pl.num_programs(0) - 1)
    def _():
        for _, grad, start, count in parts:
            for z in range(N_Z):
                row = pl.multiple_of((2 * z + core) * count, 16)
                own_terms[z, start : start + count] = grad[pl.ds(row, count), :]
                row = pl.multiple_of((2 * z + 1 - core) * count, 16)
                leaving[z, start : start + count] = grad[pl.ds(row, count), :].astype(BF16)


def mlp_both_ways(place, attended, tokens, cotangent, mods, biases, own_line, other_line):
    slot_count, length, _ = tokens.shape

    def latent(width, rows=length):
        return pl.BlockSpec((1, rows, width), lambda step, place: (step, 0, 0))

    def whole(shape):
        return pl.BlockSpec(shape, lambda step, place: (0,) * len(shape))

    line = own_line.shape
    return pl.pallas_call(
        mlp_kernel,
        grid_spec=pltpu.PrefetchScalarGridSpec(
            num_scalar_prefetch=1,
            grid=(slot_count,),
            in_specs=[latent(D), latent(D), latent(D), latent(6 * D, 1)]
            + [whole(biases.shape), whole(line), whole(line)],
            out_specs=(
                latent(D), latent(D), latent(D), latent(D, 8), latent(FF, 1), whole(line),
                whole(line), whole((D, D)),
            ),
            scratch_shapes=[
                pltpu.VMEM((D, D), BF16),
                pltpu.VMEM((FF, D), BF16),
                pltpu.VMEM((FF, D), BF16),
                pltpu.VMEM((length, FF), BF16),
                pltpu.VMEM((length, FF), F32),
                pltpu.VMEM((D, D), F32),
                pltpu.VMEM((FF, D), F32),
                pltpu.VMEM((FF, D), F32),
            ],
        ),
        out_shape=(
            jax.ShapeDtypeStruct(tokens.shape, BF16),
            jax.ShapeDtypeStruct(tokens.shape, F32),
            jax.ShapeDtypeStruct(tokens.shape, BF16),
            jax.ShapeDtypeStruct((slot_count, 8, D), F32),
            jax.ShapeDtypeStruct((slot_count, 1, FF), F32),
            jax.ShapeDtypeStruct(line, BF16),
            jax.ShapeDtypeStruct(line, F32),
            jax.ShapeDtypeStruct((D, D), BF16),
        ),
        compiler_params=pltpu.CompilerParams(vmem_limit_bytes=44 * 1024 * 1024),
        cost_estimate=pl.CostEstimate(
            flops=4_000_000_000, bytes_accessed=10_000_000, transcendentals=800_000
        ),
        name="mlp",
    )(place, attended, tokens, cotangent, mods, biases, own_line, other_line)


def combine_kernel(z_place, own, arrived, mine, one, two, three):
    for step, ref in enumerate((mine, one, two, three)):
        z = lax.rem(z_place[0] + step, N_Z)
        ref[...] = (own[z] + arrived[z].astype(F32)).astype(ref.dtype)


def combine(z_place, own, arrived):
    shape = own.shape[1:]
    whole = pl.BlockSpec(own.shape, lambda step, place: (0, 0, 0))
    part = pl.BlockSpec(shape, lambda step, place: (0, 0))
    return pl.pallas_call(
        combine_kernel,
        grid_spec=pltpu.PrefetchScalarGridSpec(
            num_scalar_prefetch=1, grid=(1,), in_specs=[whole, whole], out_specs=(part,) * 4
        ),
        out_shape=(jax.ShapeDtypeStruct(shape, F32),) + (jax.ShapeDtypeStruct(shape, BF16),) * 3,
        compiler_params=pltpu.CompilerParams(vmem_limit_bytes=20 * 1024 * 1024),
        name="combine",
    )(z_place.reshape(1), own, arrived)


def on_device(
    tokens,
    cotangent,
    labels,
    timesteps,
    counts,
    class_table,
    time_table,
    ada_weight,
    qkv_weight,
    out_weight,
    up_weight,
    down_weight,
    biases,
    ada_moment,
    qkv_moment,
    out_moment,
    up_moment,
    down_moment,
    bias_moment,
):
    slot_count, length, _ = tokens.shape
    dp_place = lax.axis_index("dp")
    z_place = dp_place // 2
    core_place = dp_place % 2

    weight_rows = [
        ada_weight.T,
        qkv_weight.T,
        out_weight.T,
        up_weight.T,
        down_weight,
    ]
    bias_shard = biases.shape[0]
    first_sent, second_shard, condition = prepare(
        labels, timesteps, class_table, time_table, weight_rows, biases
    )
    cond_act, silu_back = jax.vjp(jax.nn.silu, condition)
    cond_low = cond_act.astype(BF16)
    first_near = exchange_fsdp(first_sent)

    def cut(start, count):
        return first_near[:, start : start + count].reshape(N_FSDP * count, D)

    first_block = jnp.concatenate([cut(0, 18), cut(18, 9), cut(27, 1), cut(28, 2)], axis=0)
    second_near = gather_z(second_shard, z_place).reshape(1, N_Z * 32, D)
    second_near = exchange_fsdp(jnp.broadcast_to(second_near, (N_FSDP, N_Z * 32, D)))
    second_near = second_near.reshape(N_FSDP, N_Z, 32, D)

    def cut_line(start, count):
        rows = second_near[:, :, start : start + count].transpose(1, 0, 2, 3)
        return rows.reshape(N_Z, N_FSDP * count, D)

    first_line = gather_z(first_block, z_place)
    first_full = join_cores(first_line, swap_cores(first_line), core_place, 1)
    second_line = jnp.concatenate([cut_line(0, 3), cut_line(3, 12), cut_line(15, 12)], axis=1)

    def rows_of(full, start, count):
        return full[:, :, start : start + count].reshape(2 * N_Z * count, D)

    ada_rows = rows_of(first_full, 0, 288)
    qkv_rows = rows_of(first_full, 288, 144)
    bias_wide = rows_of(first_full, 432, 16)[:, :bias_shard].reshape(-1).astype(F32)
    cond_all = (
        first_full[:, :, 448:480]
        .reshape(N_Z, 2, N_FSDP, slot_count, D)
        .transpose(2, 0, 1, 3, 4)
        .reshape(-1, D)
    )
    bias_ada = bias_wide[: 6 * D]
    bias_query = bias_wide[6 * D : 7 * D]
    bias_value = bias_wide[7 * D : 8 * D]

    modulation = jnp.einsum("ld,kd->lk", cond_low, ada_rows, preferred_element_type=F32) + bias_ada
    pieces = jnp.split(modulation[:, None, :], 6, axis=2)
    shift_one, scale_one, gate_one, shift_two, scale_two, gate_two = pieces
    inputs = tokens.astype(F32)
    normed_one, _ = layer_norm_kept(inputs)
    attn_in = (normed_one * (1.0 + scale_one) + shift_one).astype(BF16)
    qkv_bias = jnp.concatenate([bias_query, jnp.zeros_like(bias_query), bias_value])
    packed = (times_transposed(attn_in, qkv_rows) + qkv_bias).astype(BF16)
    attended = attention(packed)
    second_other = swap_cores(second_line)
    place = jnp.stack([core_place, counts[0]])
    (
        output, grad_middle, grad_branch_low, mlp_sums, up_sums, second_leaving, second_own, out_rows,
    ) = mlp_both_ways(
        place,
        attended,
        tokens,
        cotangent,
        modulation[:, None, :],
        bias_wide[None],
        second_line,
        second_other,
    )
    second_arrived = swap_cores(second_leaving)
    rest = (out_rows, attn_in, qkv_rows, tokens, scale_one, grad_middle)
    early_qkv, early_grad, *early_sums = attention_back(0, packed, grad_branch_low, *rest)
    second_mine, *second_leaving = combine(z_place, second_own, second_arrived)
    late_scale, second_mine = lax.optimization_barrier((scale_one, second_mine))
    second_pieces = [
        shift_z(piece, step) for piece, step in zip(second_leaving, (1, 2, 3))
    ]
    rest = (out_rows, attn_in, qkv_rows, tokens, late_scale, grad_middle)
    local_qkv, input_grad, *late_sums = attention_back(
        1, packed, grad_branch_low, *rest, earlier=(early_qkv, early_grad)
    )
    shift_sum, scale_sum, query_sum, value_sum = [
        jnp.concatenate(pair, axis=0) for pair in zip(early_sums, late_sums)
    ]
    grad_gate_one, grad_shift_two, grad_scale_two, grad_gate_two = [
        mlp_sums[:, row] for row in range(4)
    ]

    def by_dp(rows):
        return rows.reshape(N_Z, 2, -1, D)

    grad_shift_one = shift_sum[:, 0]
    grad_scale_one = scale_sum[:, 0]
    grad_mod = jnp.concatenate(
        [
            grad_shift_one,
            grad_scale_one,
            grad_gate_one,
            grad_shift_two,
            grad_scale_two,
            grad_gate_two,
        ],
        axis=1,
    )
    grad_mod_low = grad_mod.astype(BF16)
    token_axes = (0, 1)
    local_bias = jnp.concatenate(
        [
            jnp.sum(grad_mod, axis=0).reshape(6, D),
            jnp.sum(query_sum, axis=token_axes)[None],
            jnp.sum(value_sum, axis=token_axes)[None],
            jnp.sum(mlp_sums[:, 4], axis=0)[None],
            jnp.sum(up_sums, axis=token_axes).reshape(FF // D, D),
            jnp.sum(mlp_sums[:, 5], axis=0)[None],
        ]
    )
    bias_terms = jnp.pad(
        local_bias.reshape(N_Z, 2, N_FSDP, bias_shard), ((0, 0),) * 3 + ((0, D - bias_shard),)
    )

    mod_rows = jnp.pad(
        grad_mod_low.reshape(slot_count, N_Z, 2, 288).transpose(1, 2, 0, 3),
        ((0, 0),) * 3 + ((0, D - 288),),
    )
    first_terms = jnp.concatenate([by_dp(local_qkv), bias_terms], axis=2)
    count_first = first_terms.shape[2]
    leaving = jnp.concatenate(
        [pick(first_terms, 1 - core_place, 1).astype(BF16), pick(mod_rows, 1 - core_place, 1)],
        axis=1,
    )
    leaving, *second_pieces = lax.optimization_barrier((leaving, *second_pieces))
    arrived = swap_cores(leaving)
    line_terms = pick(first_terms, core_place, 1) + arrived[:, :count_first].astype(F32)
    line_mod = join_cores(
        pick(mod_rows, core_place, 1), arrived[:, count_first:], core_place, 1
    ).reshape(N_Z, 2 * slot_count, D)
    line = jnp.concatenate([line_terms.astype(BF16), line_mod], axis=1)
    mods = jnp.zeros((N_Z, 2 * slot_count, 288), BF16)
    mods = lax.dynamic_update_index_in_dim(mods, pick(line_mod, z_place)[:, :288], z_place, 0)
    first_pieces = []
    for step in (1, 3, 2):
        piece = shift_z(pick(line, (z_place + step) % N_Z), step)
        first_pieces.append(piece[:count_first])
        mods = lax.dynamic_update_index_in_dim(
            mods, piece[count_first:, :288], (z_place - step) % N_Z, 0
        )
    lat_dp = 2 * N_Z * slot_count
    mod_by_shard = mods.astype(F32).reshape(lat_dp, N_FSDP, 18).transpose(1, 0, 2)
    mod_by_shard = jnp.pad(mod_by_shard.reshape(N_FSDP, 288), ((0, 0), (0, D - 288)))
    outgoing = repack(
        [pick(line_terms, z_place), *first_pieces],
        [second_mine, *second_pieces],
        mod_by_shard,
    )
    incoming = exchange_fsdp(outgoing)
    mod_all = incoming[:, 37, :288].reshape(N_FSDP * lat_dp, 18).T
    moment_rows = [ada_moment.T, qkv_moment.T, out_moment.T, up_moment.T, down_moment]
    grad_rows, new_moments, bias_row, to_owner = update_moments(
        incoming, mod_all, cond_all, moment_rows
    )
    bias_grad = bias_row[0, :bias_shard]
    block = exchange_fsdp(to_owner).reshape(N_FSDP * 24, D)
    gram = jnp.einsum("nk,nd->kd", block, block, precision=HIGH)
    third = D // 3
    top = gram[:third]
    bottom = jnp.concatenate(
        [
            gram[third : 2 * third, third : 2 * third],
            gram[third : 2 * third, 2 * third :],
            gram[2 * third :, 2 * third :],
        ],
        axis=1,
    )
    half = jnp.where(core_place == 0, top, bottom)
    half = half + swap_cores(jnp.where(core_place == 0, bottom, top))
    half = half + shift_z(half, 1) + shift_z(half, 3) + shift_z(half, 2)
    other_half = swap_cores(half)
    frames = newton_frames(
        jnp.where(core_place == 0, half, other_half),
        jnp.where(core_place == 0, other_half, half),
        block,
    )
    returned = exchange_fsdp(frames.reshape(N_FSDP, 24, D))

    new_rows = finish_weights(returned, weight_rows)

    grad_cond_act = jnp.dot(grad_mod_low, ada_rows, preferred_element_type=F32)
    cond_grad = silu_back(grad_cond_act)[0]
    bias_moment_new = MOMENTUM * bias_moment + bias_grad
    tokens_all = lax.axis_size(BOTH) * slot_count * length
    bias_new = biases - BIAS_RATE / math.sqrt(tokens_all) * bias_moment_new

    def columns(rows):
        return [rows[0].T, rows[1].T, rows[2].T, rows[3].T, rows[4]]

    return (
        output,
        input_grad,
        cond_grad,
        *columns(grad_rows),
        bias_grad,
        *columns(new_rows),
        bias_new,
        *columns(new_moments),
        bias_moment_new,
    )


def solution(mesh):
    latents = P(BOTH, None, None)
    vector = P(BOTH)
    column = P(None, BOTH)
    row = P(BOTH, None)
    matrices = (column, column, column, column, row)
    return jax.shard_map(
        on_device,
        mesh=mesh,
        in_specs=(
            latents,
            latents,
            vector,
            vector,
            vector,
            P(),
            P(),
            *matrices,
            vector,
            *matrices,
            vector,
        ),
        out_specs=(
            latents,
            latents,
            row,
            *matrices,
            vector,
            *matrices,
            vector,
            *matrices,
            vector,
        ),
        check_vma=False,
    )
```

```python
import functools
import math

import jax
import jax.numpy as jnp
from jax import lax
from jax.experimental import pallas as pl
from jax.experimental.pallas import tpu as pltpu
from jax.sharding import PartitionSpec as P

D = 384
FF = 1536
HEAD = 64
N_FSDP = 16
N_Z = 4
BOTH = ("dp", "fsdp")

MOMENTUM = 0.95
STEP_RATE = 1.2
BIAS_RATE = 0.3
EPS_NORM = 1e-06
EPS_FRAME = 1e-07
COEF_A = 3.4445
COEF_B = -4.775
COEF_C = 2.0315
HIGH = lax.Precision.HIGHEST
F32 = jnp.float32
BF16 = jnp.bfloat16


def layer_norm_kept(vectors):
    centred = vectors - jnp.mean(vectors, axis=-1, keepdims=True)
    spread = jnp.mean(centred * centred, axis=-1, keepdims=True)
    inverse = lax.rsqrt(spread + EPS_NORM)
    return (centred * inverse, inverse)


def norm_backward(grad_normed, normed, inverse):
    centred_grad = grad_normed - jnp.mean(grad_normed, axis=-1, keepdims=True)
    return inverse * (
        centred_grad - normed * jnp.mean(grad_normed * normed, axis=-1, keepdims=True)
    )


def times_transposed(left_side, rows):
    return jnp.einsum("lsd,kd->lsk", left_side, rows, preferred_element_type=F32)


def times_rows(left_side, rows):
    return jnp.einsum("lsk,kd->lsd", left_side, rows, preferred_element_type=F32)


def weight_grad_rows(grads, inputs):
    return jnp.einsum("lsk,lsd->kd", grads, inputs, preferred_element_type=F32)


def swap_cores(block):
    return lax.ppermute(block, "dp", [(d, d ^ 1) for d in range(2 * N_Z)])


def shift_z(block, step):
    pairs = [(d, ((d // 2 + step) % N_Z) * 2 + d % 2) for d in range(2 * N_Z)]
    return lax.ppermute(block, "dp", pairs)


def pick(blocks, place, axis=0):
    return lax.dynamic_index_in_dim(blocks, place, axis, keepdims=False)


def gather_z(block, z_place):
    steps = [block] + [shift_z(block, step) for step in (1, 3, 2)]
    line = jnp.zeros((N_Z,) + block.shape, block.dtype)
    for step, piece in zip((0, 1, 3, 2), steps):
        line = lax.dynamic_update_index_in_dim(line, piece, (z_place - step) % N_Z, 0)
    return line


def join_cores(own, other, core_place, axis):
    first = jnp.where(core_place == 0, own, other)
    second = jnp.where(core_place == 0, other, own)
    return jnp.stack([first, second], axis=axis)


def exchange_fsdp(blocks):
    return lax.all_to_all(blocks, "fsdp", split_axis=0, concat_axis=0, tiled=True)


def split(value):
    high = value.astype(BF16)
    return high, (value - high.astype(F32)).astype(BF16)


def times_split(left, right):
    def dot(a, b):
        return jnp.dot(a, b, preferred_element_type=F32)

    return dot(left[0], right[0]) + (dot(left[0], right[1]) + dot(left[1], right[0]))


def newton_kernel(top_ref, bottom_ref, block_ref, out_ref):
    def times(left, right):
        return jnp.dot(left, right, precision=HIGH, preferred_element_type=F32)

    third = D // 3
    top = top_ref[...]
    bottom = bottom_ref[...]
    middle = bottom[:, third : 2 * third]
    gram = jnp.concatenate(
        [
            top,
            jnp.concatenate([top[:, third : 2 * third].T, bottom[:, :third], middle], axis=1),
            jnp.concatenate([top[:, 2 * third :].T, middle.T, bottom[:, 2 * third :]], axis=1),
        ],
        axis=0,
    )
    rows = lax.broadcasted_iota(jnp.int32, (D, D), 0)
    cols = lax.broadcasted_iota(jnp.int32, (D, D), 1)
    same = rows == cols
    square_sum = jnp.sum(jnp.where(same, gram, 0.0))
    scale = 1.0 / (jnp.sqrt(square_sum) + EPS_FRAME)
    gram = gram * scale * scale
    product = None
    for sweep in range(5):
        exact = sweep < 1
        gram_parts = None if exact else split(gram)
        squared = times(gram, gram) if exact else times_split(gram_parts, gram_parts)
        step = COEF_B * gram + COEF_C * squared + jnp.where(same, COEF_A, 0.0)
        step_parts = split(step)
        if product is None:
            product = step
        else:
            product = times_split(step_parts, split(product))
        if exact:
            gram = times(times(step, gram), step)
        elif sweep < 4:
            gram = times_split(split(times_split(step_parts, gram_parts)), step_parts)
    frames = times_split(split(block_ref[...]), split(product * scale))
    out_ref[...] = frames.astype(BF16)


def newton_frames(top, bottom, block):
    return pl.pallas_call(
        newton_kernel,
        out_shape=jax.ShapeDtypeStruct((D, D), BF16),
        compiler_params=pltpu.CompilerParams(vmem_limit_bytes=16 * 1024 * 1024),
        name="newton",
    )(top, bottom, block)


SEND_ROWS = 48


def repack_kernel(
    own_first, one_first, two_first, three_first, own_second, one_second, two_second, three_second,
    mods, out_ref, first, second, stage,
):
    def total(own, *others):
        value = own[...]
        for other in others:
            value = value + other[...].astype(F32)
        return value

    first[...] = total(own_first, one_first, two_first, three_first)
    second[...] = total(own_second, one_second, two_second, three_second)
    stage[...] = jnp.zeros_like(stage)
    for place in range(N_FSDP):
        stage[0:9, :] = first[9 * place : 9 * place + 9, :]
        stage[9:12, :] = second[3 * place : 3 * place + 3, :]
        stage[12:24, :] = second[48 + 12 * place : 60 + 12 * place, :]
        stage[24:36, :] = second[240 + 12 * place : 252 + 12 * place, :]
        stage[36:37, :] = first[144 + place : 145 + place, :]
        stage[37:38, :] = mods[place : place + 1, :]
        out_ref[place] = stage[...].astype(BF16)


def repack(first_terms, second_terms, mods):
    return pl.pallas_call(
        repack_kernel,
        out_shape=jax.ShapeDtypeStruct((N_FSDP, SEND_ROWS, D), BF16),
        scratch_shapes=[
            pltpu.VMEM((160, D), F32),
            pltpu.VMEM((432, D), F32),
            pltpu.VMEM((SEND_ROWS, D), F32),
        ],
        compiler_params=pltpu.CompilerParams(vmem_limit_bytes=8 * 1024 * 1024),
        name="repack",
    )(*first_terms, *second_terms, mods)


def prep_kernel(
    labels, timesteps, class_ref, time_ref, ada, qkv, out, up, down, bias,
    first_ref, second_ref, cond_ref, stage,
):
    def looked_up(places, table):
        shape = (8, table.shape[0])
        rows = lax.broadcasted_iota(jnp.int32, shape, 0)
        entry = lax.broadcasted_iota(jnp.int32, shape, 1)
        hot = jnp.where(rows == 0, places[0], places[1]) == entry
        return jnp.dot(hot.astype(F32).astype(BF16), table[...], preferred_element_type=F32)

    condition = (looked_up(labels, class_ref) + looked_up(timesteps, time_ref))[:2]
    cond_ref[...] = condition
    stage[...] = jnp.zeros_like(stage)
    stage[0:18, :] = ada[...]
    stage[18:27, :] = qkv[...]
    stage[27:28, : bias.shape[1]] = bias[...]
    stage[28:30, :] = jax.nn.silu(condition)
    stage[32:35, :] = out[...]
    stage[35:47, :] = up[...]
    stage[47:59, :] = down[...]
    low = stage[...].astype(BF16)
    for place in range(N_FSDP):
        first_ref[place] = low[:32]
    second_ref[...] = low[32:]


def prepare(labels, timesteps, class_table, time_table, weight_rows, biases):
    scalars = pl.BlockSpec(memory_space=pltpu.SMEM)
    arrays = (class_table, time_table, *weight_rows, biases[None])
    return pl.pallas_call(
        prep_kernel,
        grid=(1,),
        out_shape=(
            jax.ShapeDtypeStruct((N_FSDP, 32, D), BF16),
            jax.ShapeDtypeStruct((32, D), BF16),
            jax.ShapeDtypeStruct((2, D), F32),
        ),
        in_specs=[scalars, scalars]
        + [pl.BlockSpec(array.shape, lambda step: (0, 0)) for array in arrays],
        out_specs=(
            pl.BlockSpec((N_FSDP, 32, D), lambda step: (0, 0, 0)),
            pl.BlockSpec((32, D), lambda step: (0, 0)),
            pl.BlockSpec((2, D), lambda step: (0, 0)),
        ),
        scratch_shapes=[pltpu.VMEM((64, D), F32)],
        compiler_params=pltpu.CompilerParams(vmem_limit_bytes=60 * 1024 * 1024),
        name="prepare",
    )(labels, timesteps, *arrays)


ROWS = (18, 9, 3, 12, 12)


def moments_kernel(incoming, mods, cond, *refs):
    old = refs[:5]
    grads = refs[5:10]
    new = refs[10:15]
    bias_ref, owner_ref = refs[15:]
    total = incoming[0].astype(F32)
    for place in range(1, N_FSDP):
        total = total + incoming[place].astype(F32)
    grads[0][...] = jnp.dot(mods[...], cond[...], preferred_element_type=F32)
    grads[1][...] = total[0:9]
    grads[2][...] = total[9:12]
    grads[3][...] = total[12:24]
    grads[4][...] = total[24:36]
    bias_ref[...] = total[36:37]
    owner_ref[...] = jnp.zeros_like(owner_ref)
    for kind in range(5):
        value = MOMENTUM * old[kind][...] + grads[kind][...]
        new[kind][...] = value
        for owner in range(kind, N_FSDP, 5):
            owner_ref[owner, 0 : ROWS[kind], :] = value


def update_moments(incoming, mods, cond, moment_rows):
    shapes = [jax.ShapeDtypeStruct((count, D), F32) for count in ROWS]
    results = pl.pallas_call(
        moments_kernel,
        out_shape=(
            *shapes,
            *shapes,
            jax.ShapeDtypeStruct((1, D), F32),
            jax.ShapeDtypeStruct((N_FSDP, 24, D), F32),
        ),
        compiler_params=pltpu.CompilerParams(vmem_limit_bytes=16 * 1024 * 1024),
        name="moments",
    )(incoming, mods, cond, *moment_rows)
    return results[:5], results[5:10], results[10], results[11]


def finish_kernel(returned, *refs):
    factors = (math.sqrt(6.0), math.sqrt(3.0), 1.0, math.sqrt(FF / D), 1.0)
    for kind in range(5):
        frame = returned[kind].astype(F32)[: ROWS[kind]]
        refs[5 + kind][...] = refs[kind][...] - STEP_RATE * factors[kind] * frame


def finish_weights(returned, weight_rows):
    return pl.pallas_call(
        finish_kernel,
        out_shape=[jax.ShapeDtypeStruct((count, D), F32) for count in ROWS],
        compiler_params=pltpu.CompilerParams(vmem_limit_bytes=8 * 1024 * 1024),
        name="finish",
    )(returned, *weight_rows)


def attention_kernel(
    core, tokens, cond, biases, own_line, other_line,
    mods_ref, attn_in, packed, attended, ada_w, qkv_w, mods,
):
    def dot(left, right, contract):
        return lax.dot_general(
            left, right, ((contract[:1], contract[1:]), ((), ())), preferred_element_type=F32
        )

    latent = pl.program_id(0)

    @pl.when(latent == 0)
    def _():
        for z in range(N_Z):
            for line, side in ((own_line, core[0]), (other_line, 1 - core[0])):
                for weight, start, count in ((ada_w, 0, 288), (qkv_w, 288, 144)):
                    row = pl.multiple_of((2 * z + side) * count, 16)
                    weight[pl.ds(row, count), :] = line[z, start : start + count]
        mods[...] = dot(cond[...], ada_w[...], (1, 1)) + biases[:, : 6 * D]

    own_mods = mods[pl.ds(latent, 1), :]
    mods_ref[0] = own_mods
    normed, _ = layer_norm_kept(tokens[0].astype(F32))
    inside = (normed * (1.0 + own_mods[:, D : 2 * D]) + own_mods[:, :D]).astype(BF16)
    attn_in[0] = inside
    query_bias = biases[:, 6 * D : 7 * D]
    value_bias = biases[:, 7 * D : 8 * D]
    for third, bias in enumerate((query_bias, None, value_bias)):
        span = slice(third * D, (third + 1) * D)
        part = dot(inside, qkv_w[span, :], (1, 1))
        packed[0, :, span] = (part if bias is None else part + bias).astype(BF16)
    score_scale = 1.0 / math.sqrt(HEAD)
    lane = lax.broadcasted_iota(jnp.int32, (packed.shape[1], 2 * HEAD), 1)
    zero = jnp.zeros((), BF16)
    for pair in range(D // (2 * HEAD)):
        start = pair * 2 * HEAD
        query = packed[0, :, start : start + 2 * HEAD]
        key = packed[0, :, D + start : D + start + 2 * HEAD]
        value = packed[0, :, 2 * D + start : 2 * D + start + 2 * HEAD]
        mixed = None
        for head in range(2):
            own = (lane >= head * HEAD) & (lane < (head + 1) * HEAD)
            scores = dot(jnp.where(own, query, zero), key, (1, 1)) * score_scale
            exponent = jnp.exp(scores - jnp.max(scores, axis=-1, keepdims=True))
            probs = exponent * (1.0 / jnp.sum(exponent, axis=-1, keepdims=True))
            term = dot(probs.astype(BF16), jnp.where(own, value, zero), (1, 0))
            mixed = term if mixed is None else mixed + term
        attended[0, :, start : start + 2 * HEAD] = mixed.astype(BF16)


def attention(core_place, tokens, cond, biases, own_line, other_line):
    slot_count, length, _ = tokens.shape

    def latent(width, rows=length):
        return pl.BlockSpec((1, rows, width), lambda step, core: (step, 0, 0))

    def whole(shape):
        return pl.BlockSpec(shape, lambda step, core: (0,) * len(shape))

    return pl.pallas_call(
        attention_kernel,
        grid_spec=pltpu.PrefetchScalarGridSpec(
            num_scalar_prefetch=1,
            grid=(slot_count,),
            in_specs=[latent(D)]
            + [whole(array.shape) for array in (cond, biases, own_line, other_line)],
            out_specs=(
                latent(6 * D, 1), latent(D), latent(3 * D), latent(D), whole((6 * D, D)),
                whole((3 * D, D)),
            ),
            scratch_shapes=[pltpu.VMEM((16, 6 * D), F32)],
        ),
        out_shape=(
            jax.ShapeDtypeStruct((slot_count, 1, 6 * D), F32),
            jax.ShapeDtypeStruct(tokens.shape, BF16),
            jax.ShapeDtypeStruct((slot_count, length, 3 * D), BF16),
            jax.ShapeDtypeStruct(tokens.shape, BF16),
            jax.ShapeDtypeStruct((6 * D, D), BF16),
            jax.ShapeDtypeStruct((3 * D, D), BF16),
        ),
        compiler_params=pltpu.CompilerParams(vmem_limit_bytes=24 * 1024 * 1024),
        cost_estimate=pl.CostEstimate(
            flops=2_000_000_000, bytes_accessed=6_000_000, transcendentals=800_000
        ),
        name="attention",
    )(core_place.reshape(1), tokens, cond, biases, own_line, other_line)


def attention_back_kernel(
    packed, branch_grad, out_rows, attn_in, qkv_rows, tokens, scale_one, middle_grad, *refs
):
    earlier = refs[0] if len(refs) == 8 else None
    qkv_grad, input_grad, shift_sum, scale_sum, query_sum, value_sum = refs[-6:]

    def dot(left, right, contract):
        return lax.dot_general(
            left, right, ((contract[:1], contract[1:]), ((), ())), preferred_element_type=F32
        )

    score_scale = 1.0 / math.sqrt(HEAD)
    attended_grad = dot(branch_grad[0], out_rows[...], (1, 0)).astype(BF16)
    lane = lax.broadcasted_iota(jnp.int32, (attended_grad.shape[0], 2 * HEAD), 1)
    inside = attn_in[0]
    zero = jnp.zeros((), BF16)
    grad_inside = None
    for pair in range(D // (2 * HEAD)):
        start = pair * 2 * HEAD
        span = slice(start, start + 2 * HEAD)
        query = packed[0, :, start : start + 2 * HEAD]
        key = packed[0, :, D + start : D + start + 2 * HEAD]
        value = packed[0, :, 2 * D + start : 2 * D + start + 2 * HEAD]
        pair_grad = attended_grad[:, span]
        sums = [None, None, None]
        for head in range(2):
            own = (lane >= head * HEAD) & (lane < (head + 1) * HEAD)
            query_own = jnp.where(own, query, zero)
            key_own = jnp.where(own, key, zero)
            grad_own = jnp.where(own, pair_grad, zero)
            scores = dot(query_own, key, (1, 1)) * score_scale
            exponent = jnp.exp(scores - jnp.max(scores, axis=-1, keepdims=True))
            probs = exponent * (1.0 / jnp.sum(exponent, axis=-1, keepdims=True))
            grad_probs = dot(grad_own, value, (1, 1))
            grad_scores = probs * (
                grad_probs - jnp.sum(grad_probs * probs, axis=-1, keepdims=True)
            )
            low_scores = grad_scores.astype(BF16)
            terms = (
                dot(low_scores, key_own, (1, 0)),
                dot(low_scores, query_own, (0, 0)),
                dot(probs.astype(BF16), grad_own, (0, 0)),
            )
            sums = [term if old is None else old + term for old, term in zip(sums, terms)]
        grad_query = sums[0] * score_scale
        grad_key = sums[1] * score_scale
        query_sum[0, :, span] = jnp.sum(grad_query, axis=0, keepdims=True)
        value_sum[0, :, span] = jnp.sum(sums[2], axis=0, keepdims=True)
        for third, part in enumerate((grad_query, grad_key, sums[2])):
            part = part.astype(BF16)
            place = slice(third * D + start, third * D + start + 2 * HEAD)
            term = dot(part, inside, (0, 0))
            qkv_grad[place, :] = term if earlier is None else earlier[place, :] + term
            back = dot(part, qkv_rows[place, :], (1, 0))
            grad_inside = back if grad_inside is None else grad_inside + back
    normed, inverse = layer_norm_kept(tokens[0].astype(F32))
    shift_sum[0] = jnp.sum(grad_inside, axis=0, keepdims=True)
    scale_sum[0] = jnp.sum(grad_inside * normed, axis=0, keepdims=True)
    input_grad[0] = middle_grad[0] + norm_backward(
        grad_inside * (1.0 + scale_one[0]), normed, inverse
    )


def attention_back(
    which, packed, branch_grad, out_rows, attn_in, qkv_rows, tokens, scale_one, middle_grad,
    earlier=(),
):
    _, length, _ = tokens.shape

    def latent(width, rows=length):
        return pl.BlockSpec((1, rows, width), lambda step: (which, 0, 0))

    def whole(rows):
        return pl.BlockSpec((rows, D), lambda step: (0, 0))

    one = pl.BlockSpec((1, 1, D), lambda step: (0, 0, 0))
    small = jax.ShapeDtypeStruct((1, 1, D), F32)
    return pl.pallas_call(
        attention_back_kernel,
        grid=(1,),
        out_shape=(
            jax.ShapeDtypeStruct((3 * D, D), F32),
            jax.ShapeDtypeStruct(tokens.shape, F32),
            small,
            small,
            small,
            small,
        ),
        in_specs=[
            latent(3 * D), latent(D), whole(D), latent(D), whole(3 * D), latent(D), latent(D, 1),
            latent(D),
        ]
        + ([whole(3 * D), pl.BlockSpec(memory_space=pl.ANY)] if earlier else []),
        out_specs=(whole(3 * D), latent(D), one, one, one, one),
        input_output_aliases={9: 1} if earlier else {},
        compiler_params=pltpu.CompilerParams(vmem_limit_bytes=24 * 1024 * 1024),
        cost_estimate=pl.CostEstimate(
            flops=1_800_000_000, bytes_accessed=5_000_000, transcendentals=400_000
        ),
        name="attention_back",
    )(packed, branch_grad, out_rows, attn_in, qkv_rows, tokens, scale_one, middle_grad, *earlier)


def mlp_kernel(
    place, attended, tokens, cotangent, mods, biases, own_line, other_line,
    output, middle_grad, branch_grad, sums, up_sum, leaving, own_terms,
    out_rows, out_w, up_w, down_w, hidden, slope, out_g, up_g, down_g,
):
    def dot(left, right, contract):
        return lax.dot_general(
            left, right, ((contract[:1], contract[1:]), ((), ())), preferred_element_type=F32
        )

    latent = pl.program_id(0)
    core = place[0]
    parts = ((out_w, out_g, 0, 48), (up_w, up_g, 48, 192), (down_w, down_g, 240, 192))

    @pl.when(latent == 0)
    def _():
        for weight, grad, start, count in parts:
            for z in range(N_Z):
                for line, side in ((own_line, core), (other_line, 1 - core)):
                    row = pl.multiple_of((2 * z + side) * count, 16)
                    weight[pl.ds(row, count), :] = line[z, start : start + count]
            grad[...] = jnp.zeros_like(grad)
        out_rows[...] = out_w[...]

    shift_two, scale_two, gate_one, gate_two = [
        mods[0, :, part * D : (part + 1) * D] for part in (3, 4, 2, 5)
    ]
    bias_out = biases[:, 8 * D : 9 * D]
    bias_up = biases[:, 9 * D : 9 * D + FF]
    bias_down = biases[:, 9 * D + FF :]
    attended_low = attended[0]
    branch = dot(attended_low, out_w[...], (1, 1)) + bias_out
    middle = tokens[0].astype(F32) + gate_one * branch
    normed, inverse = layer_norm_kept(middle)
    mlp_in = (normed * (1.0 + scale_two) + shift_two).astype(BF16)
    chunk = 512
    result = bias_down
    for start in range(0, FF, chunk):
        span = slice(start, start + chunk)
        before = dot(mlp_in, up_w[span, :], (1, 1)) + bias_up[:, span]
        square = before * before
        slant = math.sqrt(2.0 / math.pi)
        bend = jnp.tanh(before * (slant + slant * 0.044715 * square))
        share = 0.5 + 0.5 * bend
        low = (before * share).astype(BF16)
        hidden[:, span] = low
        slope[:, span] = share + before * (0.5 - 0.5 * bend * bend) * (
            slant + 3.0 * slant * 0.044715 * square
        )
        result = result + dot(low, down_w[span, :], (1, 0))
    live = latent < place[1]
    output[0] = jnp.where(live, middle + gate_two * result, 0.0).astype(BF16)
    grad_out = jnp.where(live, cotangent[0].astype(F32), 0.0)
    grad_result = grad_out * gate_two
    result_low = grad_result.astype(BF16)
    grad_in = None
    for start in range(0, FF, chunk):
        span = slice(start, start + chunk)
        down_g[span, :] += dot(hidden[:, span], result_low, (0, 0))
        grad_before = dot(result_low, down_w[span, :], (1, 1)) * slope[:, span]
        up_sum[0, :, span] = jnp.sum(grad_before, axis=0, keepdims=True)
        low = grad_before.astype(BF16)
        up_g[span, :] += dot(low, mlp_in, (0, 0))
        back = dot(low, up_w[span, :], (1, 0))
        grad_in = back if grad_in is None else grad_in + back
    grad_middle = grad_out + norm_backward(grad_in * (1.0 + scale_two), normed, inverse)
    grad_branch = grad_middle * gate_one
    branch_low = grad_branch.astype(BF16)
    out_g[...] += dot(branch_low, attended_low, (0, 0))
    middle_grad[0] = grad_middle
    branch_grad[0] = branch_low
    totals = (
        grad_middle * branch, grad_in, grad_in * normed, grad_out * result, grad_branch, grad_result,
    )
    for row, terms in enumerate(totals):
        sums[0, row : row + 1, :] = jnp.sum(terms, axis=0, keepdims=True)

    @pl.when(latent == pl.num_programs(0) - 1)
    def _():
        for _, grad, start, count in parts:
            for z in range(N_Z):
                row = pl.multiple_of((2 * z + core) * count, 16)
                own_terms[z, start : start + count] = grad[pl.ds(row, count), :]
                row = pl.multiple_of((2 * z + 1 - core) * count, 16)
                leaving[z, start : start + count] = grad[pl.ds(row, count), :].astype(BF16)


def mlp_both_ways(place, attended, tokens, cotangent, mods, biases, own_line, other_line):
    slot_count, length, _ = tokens.shape

    def latent(width, rows=length):
        return pl.BlockSpec((1, rows, width), lambda step, place: (step, 0, 0))

    def whole(shape):
        return pl.BlockSpec(shape, lambda step, place: (0,) * len(shape))

    line = own_line.shape
    return pl.pallas_call(
        mlp_kernel,
        grid_spec=pltpu.PrefetchScalarGridSpec(
            num_scalar_prefetch=1,
            grid=(slot_count,),
            in_specs=[latent(D), latent(D), latent(D), latent(6 * D, 1)]
            + [whole(biases.shape), whole(line), whole(line)],
            out_specs=(
                latent(D), latent(D), latent(D), latent(D, 8), latent(FF, 1), whole(line),
                whole(line), whole((D, D)),
            ),
            scratch_shapes=[
                pltpu.VMEM((D, D), BF16),
                pltpu.VMEM((FF, D), BF16),
                pltpu.VMEM((FF, D), BF16),
                pltpu.VMEM((length, FF), BF16),
                pltpu.VMEM((length, FF), F32),
                pltpu.VMEM((D, D), F32),
                pltpu.VMEM((FF, D), F32),
                pltpu.VMEM((FF, D), F32),
            ],
        ),
        out_shape=(
            jax.ShapeDtypeStruct(tokens.shape, BF16),
            jax.ShapeDtypeStruct(tokens.shape, F32),
            jax.ShapeDtypeStruct(tokens.shape, BF16),
            jax.ShapeDtypeStruct((slot_count, 8, D), F32),
            jax.ShapeDtypeStruct((slot_count, 1, FF), F32),
            jax.ShapeDtypeStruct(line, BF16),
            jax.ShapeDtypeStruct(line, F32),
            jax.ShapeDtypeStruct((D, D), BF16),
        ),
        compiler_params=pltpu.CompilerParams(vmem_limit_bytes=34 * 1024 * 1024),
        cost_estimate=pl.CostEstimate(
            flops=4_000_000_000, bytes_accessed=10_000_000, transcendentals=800_000
        ),
        name="mlp",
    )(place, attended, tokens, cotangent, mods, biases, own_line, other_line)


def combine_kernel(z_place, own, arrived, mine, one, two, three):
    for step, ref in enumerate((mine, one, two, three)):
        z = lax.rem(z_place[0] + step, N_Z)
        ref[...] = (own[z] + arrived[z].astype(F32)).astype(ref.dtype)


def combine(z_place, own, arrived):
    shape = own.shape[1:]
    whole = pl.BlockSpec(own.shape, lambda step, place: (0, 0, 0))
    part = pl.BlockSpec(shape, lambda step, place: (0, 0))
    return pl.pallas_call(
        combine_kernel,
        grid_spec=pltpu.PrefetchScalarGridSpec(
            num_scalar_prefetch=1, grid=(1,), in_specs=[whole, whole], out_specs=(part,) * 4
        ),
        out_shape=(jax.ShapeDtypeStruct(shape, F32),) + (jax.ShapeDtypeStruct(shape, BF16),) * 3,
        compiler_params=pltpu.CompilerParams(vmem_limit_bytes=20 * 1024 * 1024),
        name="combine",
    )(z_place.reshape(1), own, arrived)


def on_device(
    tokens,
    cotangent,
    labels,
    timesteps,
    counts,
    class_table,
    time_table,
    ada_weight,
    qkv_weight,
    out_weight,
    up_weight,
    down_weight,
    biases,
    ada_moment,
    qkv_moment,
    out_moment,
    up_moment,
    down_moment,
    bias_moment,
):
    slot_count, length, _ = tokens.shape
    dp_place = lax.axis_index("dp")
    z_place = dp_place // 2
    core_place = dp_place % 2

    weight_rows = [
        ada_weight.T,
        qkv_weight.T,
        out_weight.T,
        up_weight.T,
        down_weight,
    ]
    bias_shard = biases.shape[0]
    first_sent, second_shard, condition = prepare(
        labels, timesteps, class_table, time_table, weight_rows, biases
    )
    cond_act, silu_back = jax.vjp(jax.nn.silu, condition)
    cond_low = cond_act.astype(BF16)
    first_near = exchange_fsdp(first_sent)

    def cut(start, count):
        return first_near[:, start : start + count].reshape(N_FSDP * count, D)

    first_block = jnp.concatenate([cut(0, 18), cut(18, 9), cut(27, 1), cut(28, 2)], axis=0)
    second_near = gather_z(second_shard, z_place).reshape(1, N_Z * 32, D)
    second_near = exchange_fsdp(jnp.broadcast_to(second_near, (N_FSDP, N_Z * 32, D)))
    second_near = second_near.reshape(N_FSDP, N_Z, 32, D)

    def cut_line(start, count):
        rows = second_near[:, :, start : start + count].transpose(1, 0, 2, 3)
        return rows.reshape(N_Z, N_FSDP * count, D)

    first_line = gather_z(first_block, z_place)
    first_other = swap_cores(first_line)
    second_line = jnp.concatenate([cut_line(0, 3), cut_line(3, 12), cut_line(15, 12)], axis=1)

    small_rows = join_cores(first_line[:, 432:], first_other[:, 432:], core_place, 1)
    bias_wide = small_rows[:, :, :16, :bias_shard].reshape(1, -1).astype(F32)
    cond_all = (
        small_rows[:, :, 16:]
        .reshape(N_Z, 2, N_FSDP, slot_count, D)
        .transpose(2, 0, 1, 3, 4)
        .reshape(-1, D)
    )
    modulation, attn_in, packed, attended, ada_rows, qkv_rows = attention(
        core_place,
        tokens,
        jnp.pad(cond_low, ((0, 16 - slot_count), (0, 0))),
        bias_wide,
        first_line,
        first_other,
    )
    scale_one = modulation[:, :, D : 2 * D]
    second_other = swap_cores(second_line)
    place = jnp.stack([core_place, counts[0]])
    (
        output, grad_middle, grad_branch_low, mlp_sums, up_sums, second_leaving, second_own, out_rows,
    ) = mlp_both_ways(
        place,
        attended,
        tokens,
        cotangent,
        modulation,
        bias_wide,
        second_line,
        second_other,
    )
    second_arrived = swap_cores(second_leaving)
    rest = (out_rows, attn_in, qkv_rows, tokens, scale_one, grad_middle)
    early_qkv, early_grad, *early_sums = attention_back(0, packed, grad_branch_low, *rest)
    second_mine, *second_leaving = combine(z_place, second_own, second_arrived)
    late_scale, second_mine = lax.optimization_barrier((scale_one, second_mine))
    second_pieces = [
        shift_z(piece, step) for piece, step in zip(second_leaving, (1, 2, 3))
    ]
    rest = (out_rows, attn_in, qkv_rows, tokens, late_scale, grad_middle)
    local_qkv, input_grad, *late_sums = attention_back(
        1, packed, grad_branch_low, *rest, earlier=(early_qkv, early_grad)
    )
    shift_sum, scale_sum, query_sum, value_sum = [
        jnp.concatenate(pair, axis=0) for pair in zip(early_sums, late_sums)
    ]
    grad_gate_one, grad_shift_two, grad_scale_two, grad_gate_two = [
        mlp_sums[:, row] for row in range(4)
    ]

    def by_dp(rows):
        return rows.reshape(N_Z, 2, -1, D)

    grad_shift_one = shift_sum[:, 0]
    grad_scale_one = scale_sum[:, 0]
    grad_mod = jnp.concatenate(
        [
            grad_shift_one,
            grad_scale_one,
            grad_gate_one,
            grad_shift_two,
            grad_scale_two,
            grad_gate_two,
        ],
        axis=1,
    )
    grad_mod_low = grad_mod.astype(BF16)
    token_axes = (0, 1)
    local_bias = jnp.concatenate(
        [
            jnp.sum(grad_mod, axis=0).reshape(6, D),
            jnp.sum(query_sum, axis=token_axes)[None],
            jnp.sum(value_sum, axis=token_axes)[None],
            jnp.sum(mlp_sums[:, 4], axis=0)[None],
            jnp.sum(up_sums, axis=token_axes).reshape(FF // D, D),
            jnp.sum(mlp_sums[:, 5], axis=0)[None],
        ]
    )
    bias_terms = jnp.pad(
        local_bias.reshape(N_Z, 2, N_FSDP, bias_shard), ((0, 0),) * 3 + ((0, D - bias_shard),)
    )

    mod_rows = jnp.pad(
        grad_mod_low.reshape(slot_count, N_Z, 2, 288).transpose(1, 2, 0, 3),
        ((0, 0),) * 3 + ((0, D - 288),),
    )
    first_terms = jnp.concatenate([by_dp(local_qkv), bias_terms], axis=2)
    count_first = first_terms.shape[2]
    leaving = jnp.concatenate(
        [pick(first_terms, 1 - core_place, 1).astype(BF16), pick(mod_rows, 1 - core_place, 1)],
        axis=1,
    )
    leaving, *second_pieces = lax.optimization_barrier((leaving, *second_pieces))
    arrived = swap_cores(leaving)
    line_terms = pick(first_terms, core_place, 1) + arrived[:, :count_first].astype(F32)
    line_mod = join_cores(
        pick(mod_rows, core_place, 1), arrived[:, count_first:], core_place, 1
    ).reshape(N_Z, 2 * slot_count, D)
    line = jnp.concatenate([line_terms.astype(BF16), line_mod], axis=1)
    mods = jnp.zeros((N_Z, 2 * slot_count, 288), BF16)
    mods = lax.dynamic_update_index_in_dim(mods, pick(line_mod, z_place)[:, :288], z_place, 0)
    first_pieces = []
    for step in (1, 3, 2):
        piece = shift_z(pick(line, (z_place + step) % N_Z), step)
        first_pieces.append(piece[:count_first])
        mods = lax.dynamic_update_index_in_dim(
            mods, piece[count_first:, :288], (z_place - step) % N_Z, 0
        )
    lat_dp = 2 * N_Z * slot_count
    mod_by_shard = mods.astype(F32).reshape(lat_dp, N_FSDP, 18).transpose(1, 0, 2)
    mod_by_shard = jnp.pad(mod_by_shard.reshape(N_FSDP, 288), ((0, 0), (0, D - 288)))
    outgoing = repack(
        [pick(line_terms, z_place), *first_pieces],
        [second_mine, *second_pieces],
        mod_by_shard,
    )
    incoming = exchange_fsdp(outgoing)
    mod_all = incoming[:, 37, :288].reshape(N_FSDP * lat_dp, 18).T
    moment_rows = [ada_moment.T, qkv_moment.T, out_moment.T, up_moment.T, down_moment]
    grad_rows, new_moments, bias_row, to_owner = update_moments(
        incoming, mod_all, cond_all, moment_rows
    )
    bias_grad = bias_row[0, :bias_shard]
    block = exchange_fsdp(to_owner).reshape(N_FSDP * 24, D)
    gram = jnp.einsum("nk,nd->kd", block, block, precision=HIGH)
    third = D // 3
    top = gram[:third]
    bottom = jnp.concatenate(
        [
            gram[third : 2 * third, third : 2 * third],
            gram[third : 2 * third, 2 * third :],
            gram[2 * third :, 2 * third :],
        ],
        axis=1,
    )
    half = jnp.where(core_place == 0, top, bottom)
    half = half + swap_cores(jnp.where(core_place == 0, bottom, top))
    half = half + shift_z(half, 1) + shift_z(half, 3) + shift_z(half, 2)
    other_half = swap_cores(half)
    frames = newton_frames(
        jnp.where(core_place == 0, half, other_half),
        jnp.where(core_place == 0, other_half, half),
        block,
    )
    returned = exchange_fsdp(frames.reshape(N_FSDP, 24, D))

    new_rows = finish_weights(returned, weight_rows)

    grad_cond_act = jnp.dot(grad_mod_low, ada_rows, preferred_element_type=F32)
    cond_grad = silu_back(grad_cond_act)[0]
    bias_moment_new = MOMENTUM * bias_moment + bias_grad
    tokens_all = lax.axis_size(BOTH) * slot_count * length
    bias_new = biases - BIAS_RATE / math.sqrt(tokens_all) * bias_moment_new

    def columns(rows):
        return [rows[0].T, rows[1].T, rows[2].T, rows[3].T, rows[4]]

    return (
        output,
        input_grad,
        cond_grad,
        *columns(grad_rows),
        bias_grad,
        *columns(new_rows),
        bias_new,
        *columns(new_moments),
        bias_moment_new,
    )


def solution(mesh):
    latents = P(BOTH, None, None)
    vector = P(BOTH)
    column = P(None, BOTH)
    row = P(BOTH, None)
    matrices = (column, column, column, column, row)
    return jax.shard_map(
        on_device,
        mesh=mesh,
        in_specs=(
            latents,
            latents,
            vector,
            vector,
            vector,
            P(),
            P(),
            *matrices,
            vector,
            *matrices,
            vector,
        ),
        out_specs=(
            latents,
            latents,
            row,
            *matrices,
            vector,
            *matrices,
            vector,
            *matrices,
            vector,
        ),
        check_vma=False,
    )
```
